256 devices in a mesh: rep: 16 (over y, x_lo, core), gz: 16 (over z, x_hi).
Axes of the slice: x: 4 (x_hi: 2, x_lo: 2; x = x_hi * 2 + x_lo), y: 4, z: 8, core: 2. Of those that a mesh axis runs over, the one named last changes fastest.
Arguments:
- field: float32 [16, 64, 256, 256], P('rep', 'gz'), may hold values from -4 to 4
- momenta: float32 [16, 64, 256, 256], P('rep', 'gz'), may hold values from -6 to 6
- counts: int32 [16], replicated, may hold values from 0 to 9, as said below
- accept: int32 [16], P('rep'), may hold values 0 or 1
Outputs:
- new_field: float32 [16, 64, 256, 256], P('rep', 'gz')
The draws below stay inside these ranges and needn't reach their ends.
Inputs may be any that keep to these rules, and one draw needn't show every extreme that they name: counts sum to 16; exactly one replica has the largest count, 9; every other count is 0 or 1.
All inputs are finite; a program needn't handle non-finite values. No bound on the sum of `accept` on one device may be relied on, other than what follows from the above.
Results may differ from the reference program's by a relative error of at most 0.0003.
Values sent between devices are 32-bit elements; how exact they have to be, the bound alone decides.
A program may use at most 64 MiB of HBM per device.

```python
import jax
import jax.numpy as jnp
from jax import lax

LX = 256
LY = 256
STEPS = 4
R = 16
LZ = 64


def draw_counts(key, part):
    key = jax.random.fold_in(key, 11)
    first, second = jax.random.split(key, 2)
    half = R // 2
    place = jax.random.randint(first, (), 0, half).astype(jnp.int32)
    index = jnp.arange(R, dtype=jnp.int32)
    order = jax.random.permutation(second, R).astype(jnp.int32)
    after = index > place
    beaten = jnp.sum((after[None, :] & (order[None, :] < order[:, None])).astype(jnp.int32), axis=1)
    empty = after & (beaten < half)
    result = jnp.where(index < place, 1, jnp.where(index == place, half + 1, jnp.where(empty, 0, 1)))
    return result.astype(jnp.int32)


def touch_ends(values, key, smallest, largest):
    longest = values.shape.index(max(values.shape))
    spots = []
    for shift in (0, 1):
        where = [jax.random.randint(jax.random.fold_in(key, axis), (), 0, length) for axis, length in enumerate(values.shape)]
        where[longest] = (where[longest] + shift) % values.shape[longest]
        spots.append(tuple(where))
    return values.at[spots[0]].set(smallest).at[spots[1]].set(largest)


def levels(key, extent, shards, least, largest):
    gain, own = 1.0, jax.random.fold_in(key, 6)
    for dim, blocks in shards:
        heights = jnp.exp(jax.random.uniform(jax.random.fold_in(own, dim), (blocks,), jnp.float32, least / len(shards), largest / len(shards)))
        gain = gain * jnp.repeat(heights, extent[dim] // blocks).reshape([-1 if axis == dim else 1 for axis in range(len(extent))])
    return gain


def centred(rng, dims, deviation, bound, cuts=(), kind=jnp.bfloat16):
    drawn = deviation * jax.random.normal(rng, dims, jnp.float32)
    if cuts:
        drawn = drawn * levels(rng, dims, cuts, -0.22, 0.18)
    return jnp.clip(drawn, -bound, bound).astype(kind)


def setup_inputs(seed: int = 0) -> dict:
    key_list = jax.random.split(jax.random.key(seed), 5)
    return {
        "field": centred(key_list[0], (R, LZ, LY, LX), 0.8, 4.0, ((0, 16), (1, 16)), jnp.float32),
        "momenta": centred(key_list[1], (R, LZ, LY, LX), 1.0, 6.0, ((0, 16), (1, 16)), jnp.float32),
        "counts": draw_counts(jax.random.fold_in(key_list[4], 71), 0),
        "accept": touch_ends((jax.random.randint(key_list[3], (R,), 0, 4) < 3).astype(jnp.int32), jax.random.fold_in(key_list[3], 1), 0, 1),
    }


KAPPA = 0.16
LAMBDA = 0.015
EPS = 0.75


def parent_table(counts):
    cum = jnp.cumsum(counts).astype(jnp.int32)
    slots = jnp.arange(counts.shape[0], dtype=jnp.int32)
    return jnp.sum((cum[None, :] <= slots[:, None]).astype(jnp.int32), axis=1).astype(jnp.int32)


def force(phi):
    beside_all = jnp.zeros_like(phi)
    for axis in range(3):
        beside_all = beside_all + jnp.roll(phi, 1, axis) + jnp.roll(phi, -1, axis)
    return 2.0 * KAPPA * beside_all - 2.0 * phi - 4.0 * LAMBDA * phi * (phi * phi - 1.0)


def trajectory(phi, mom):
    mom = mom + 0.5 * EPS * force(phi)
    for step in range(STEPS):
        phi = phi + EPS * mom
        if step < STEPS - 1:
            mom = mom + EPS * force(phi)
    return phi


def reference(field, momenta, counts, accept):
    parents = parent_table(counts)

    def one_slot(items):
        parent, mom, flag = items
        start = field[parent]
        moved = trajectory(start, mom)
        return jnp.where(flag == 1, moved, start)

    return lax.map(one_slot, (parents, momenta, accept))
```

```python
import jax
import jax.numpy as jnp
from jax import lax
from jax.experimental import pallas as pl
from jax.experimental.pallas import tpu as pltpu
from jax.sharding import PartitionSpec as P

STEPS = 4
KAPPA = 0.16
LAMBDA = 0.015
EPS = 0.75

MESH = pl.DeviceIdType.MESH
SLOTS = 4
ROWS = 32
PAD = 8
ALL = ROWS + 2 * PAD
LANES = 256
PAIRS = 4
CHUNKS = 16
LAG = 2
MESSAGES = CHUNKS + LAG
ORDER = (0, 2, 1, 3)


def kernel(field, momenta, counts, accept, out, own, send_up, send_down, from_below, from_above, phi0, phi1, phi2, phi3, mom,
           done, flag, flags, a_ss, a_rs, c_ss, c_rs, f_ss, f_rs, up_ss, up_rs, down_ss, down_rs, z_ss, z_rs, zm_ss, zm_rs,
           r_ss, r_rs, rz_ss, rz_rs, d_ss, d_rs, e_ss, e_rs, here):
    rep, gz = lax.axis_index("rep"), lax.axis_index("gz")
    y, z = rep // 4, gz // 2
    q = (gz % 2) * 4 + rep % 4
    slot, half = rep % 4, gz % 2

    def place(ring, row, depth):
        return (row * 4 + ring % 4, depth * 2 + ring // 4)

    def ring(step):
        return place((q + step + 8) % 8, y, z)

    above, below = place(q, (y + 1) % 4, z), place(q, (y + 3) % 4, z)
    z_next, z_last = place(q, y, (z + 1) % 8), place(q, y, (z + 7) % 8)

    def remote(src, dst, ss, rs, device):
        return pltpu.make_async_remote_copy(src_ref=src, dst_ref=dst, send_sem=ss, recv_sem=rs, device_id=device, device_id_type=MESH)

    barrier = pltpu.get_barrier_semaphore()
    partners = [ring(step) for step in range(1, 8)] + [above, below, z_next, z_last]
    for device in partners:
        pl.semaphore_signal(barrier, inc=1, device_id=device, device_id_type=MESH)
    pl.semaphore_wait(barrier, len(partners))

    def rows_of(place_):
        return pl.ds(pl.multiple_of(place_ * ROWS, ROWS), ROWS)

    def local_plane(pair):
        return pair + half * (3 - 2 * pair)

    def field_copy(pair, step):
        src = field.at[0, local_plane(pair), rows_of((q + step) % 8)]
        dst = own.at[pair, half, slot]
        if step == 0:
            return pltpu.make_async_copy(src, dst, a_rs.at[pair, 0])
        return remote(src, dst, a_ss.at[pair, step], a_rs.at[pair, step], ring(step))

    def momenta_copy(pair, step):
        src = momenta.at[0, local_plane(pair), rows_of((q + step) % 8)]
        dst = mom.at[slot, 4 + half * 4 + local_plane(pair)]
        if step == 0:
            return pltpu.make_async_copy(src, dst, c_rs.at[pair, 0])
        return remote(src, dst, c_ss.at[pair, step], c_rs.at[pair, step], ring(step))

    def flag_copy(step):
        if step == 0:
            return pltpu.make_async_copy(flag, flags.at[q], f_rs.at[0])
        return remote(flag, flags.at[q], f_ss.at[step], f_rs.at[step], ring(step))

    for pair in range(PAIRS):
        for step in range(8):
            field_copy(pair, step).start()
    flag[...] = jnp.full(flag.shape, accept[0], jnp.int32)
    for step in range(8):
        flag_copy(step).start()

    alive = [[(counts[4 * ((y + d) % 4) + i] > 0).astype(jnp.int32) for i in range(4)] for d in range(4)]
    before = [[sum(alive[d][:i], jnp.int32(0)) for i in range(4)] for d in range(4)]
    total = [sum(alive[d], jnp.int32(0)) for d in range(4)]
    mine = [jnp.int32(-1)] * 4
    for c in range(4):
        for i in range(4):
            mine[c] = jnp.where((alive[0][i] == 1) & (before[0][i] == c), i, mine[c])
    split_up = jnp.minimum(total[3], 4 - total[2])
    split = jnp.minimum(total[2], 4 - total[1])
    cum, parent = jnp.int32(0), [jnp.int32(0)] * SLOTS
    for r in range(16):
        cum = cum + counts[r]
        for s in range(SLOTS):
            parent[s] = parent[s] + (cum <= 4 * y + s).astype(jnp.int32)
    code = []
    for s in range(SLOTS):
        value = jnp.int32(0)
        for d in range(4):
            for i in range(4):
                k = before[d][i]
                if d == 0:
                    way = jnp.int32(i)
                elif d == 1:
                    way = 4 + k
                elif d == 3:
                    way = 8 + k
                else:
                    way = jnp.where(k < split, 12 + total[1] + k, 16 + total[3] + k - split)
                value = jnp.where(parent[s] == 4 * ((y + d) % 4) + i, way, value)
        code.append(value)

    def same(value, number):
        return jnp.full((8, LANES), value, jnp.int32) == number

    def octet(t):
        return t // 4, pl.ds(pl.multiple_of((t % 4) * 8, 8), 8)

    def assemble(t, forward):
        pair, rows = octet(jnp.minimum(t, CHUNKS - 1))
        for c in range(4):
            own_here = [same(mine[c], i) for i in range(4)]
            down_here = [same(total[0], c - f) for f in range(c + 1)]
            up_here = [same(split_up + c - total[0], f) for f in range(4)]
            for h in range(2):
                pieces = [own[pair, h, i, rows, :] for i in range(4)]
                if forward:
                    down, up = from_above[t - LAG, 0, h], from_below[t - LAG, 0, h]
                    for f in range(1, c + 1):
                        down = jnp.where(down_here[f], from_above[t - LAG, f, h], down)
                    for f in range(1, 4):
                        up = jnp.where(up_here[f], from_below[t - LAG, f, h], up)
                else:
                    down = up = pieces[0]
                for i in range(4):
                    down = jnp.where(own_here[i], pieces[i], down)
                    up = jnp.where(own_here[i], pieces[i], up)
                send_down[t, c, h] = down
                send_up[t, c, h] = up

    def up_copy(t):
        return remote(send_up.at[t], from_below.at[t], up_ss.at[t], up_rs.at[t], above)

    def down_copy(t):
        return remote(send_down.at[t], from_above.at[t], down_ss.at[t], down_rs.at[t], below)

    def pick(u):
        pair, rows = octet(u)
        target = pl.ds(pl.multiple_of(PAD + (u % 4) * 8, 8), 8)
        for s in range(SLOTS):
            here_ = [same(code[s], k) for k in range(20)]
            for h in range(2):
                value = own[pair, h, 0, rows, :]
                for i in range(1, 4):
                    value = jnp.where(here_[i], own[pair, h, i, rows, :], value)
                for c in range(4):
                    value = jnp.where(here_[4 + c], from_above[u, c, h], value)
                    value = jnp.where(here_[8 + c], from_below[u, c, h], value)
                    value = jnp.where(here_[12 + c], from_above[u + LAG, c, h], value)
                    value = jnp.where(here_[16 + c], from_below[u + LAG, c, h], value)
                plane = 4 + pair if h == 0 else 11 - pair
                phi0[s, plane, target, :] = value

    inner = pl.ds(PAD, ROWS)
    first, last = pl.ds(PAD, PAD), pl.ds(ROWS, PAD)
    low, high = pl.ds(0, PAD), pl.ds(PAD + ROWS, PAD)

    def z_copies(pair):
        return (
            remote(phi0.at[:, 4 + pair, inner], phi0.at[:, 12 + pair, inner], z_ss.at[pair, 0], z_rs.at[pair, 0], z_last),
            remote(phi0.at[:, 11 - pair, inner], phi0.at[:, 3 - pair, inner], z_ss.at[pair, 1], z_rs.at[pair, 1], z_next),
        )

    def zm_copies(pair):
        return (
            remote(mom.at[:, 4 + pair], mom.at[:, 12 + pair], zm_ss.at[pair, 0], zm_rs.at[pair, 0], z_last),
            remote(mom.at[:, 11 - pair], mom.at[:, 3 - pair], zm_ss.at[pair, 1], zm_rs.at[pair, 1], z_next),
        )

    def row_copies(planes, ss, rs):
        copies = []
        for n, plane in enumerate(planes):
            copies.append(remote(phi0.at[:, plane, first], phi0.at[:, plane, high], ss.at[n, 0], rs.at[n, 0], ring(-1)))
            copies.append(remote(phi0.at[:, plane, last], phi0.at[:, plane, low], ss.at[n, 1], rs.at[n, 1], ring(1)))
        return copies

    def own_rows(pair):
        return row_copies((4 + pair, 11 - pair), r_ss.at[pair], r_rs.at[pair])

    def halo_rows(pair):
        return row_copies((12 + pair, 3 - pair), rz_ss.at[pair], rz_rs.at[pair])

    def tick(t, carry):
        @pl.when((t % 4 == 0) & (t < CHUNKS))
        def _():
            for step in range(8):
                copy = field_copy(t // 4, step)
                copy.wait() if step == 0 else copy.wait_recv()

        @pl.when(t >= LAG)
        def _():
            up_copy(t - LAG).wait_recv()
            down_copy(t - LAG).wait_recv()

        @pl.when(t < LAG)
        def _():
            assemble(t, False)

        @pl.when((t >= LAG) & (t < MESSAGES))
        def _():
            assemble(t, True)

        @pl.when(t < MESSAGES)
        def _():
            up_copy(t).start()
            down_copy(t).start()

        @pl.when((t >= 6) & (t < 14) & (t % 2 == 0))
        def _():
            for step in range(8):
                momenta_copy((t - 6) // 2, step).start()

        @pl.when(t >= 2 * LAG)
        def _():
            pick(t - 2 * LAG)

        @pl.when((t >= 7) & (t % 4 == 3))
        def _():
            for copy in z_copies((t - 7) // 4) + tuple(own_rows((t - 7) // 4)):
                copy.start()

        @pl.when((t == 11) | (t == 13) | (t == 15))
        def _():
            pair = (t - 11) // 2
            for step in range(8):
                copy = momenta_copy(pair, step)
                copy.wait() if step == 0 else copy.wait_recv()
            for copy in zm_copies(pair):
                copy.start()

        @pl.when((t == 10) | (t == 14) | (t == 18))
        def _():
            pair = (t - 10) // 4
            for copy in z_copies(pair):
                copy.wait_recv()
            for copy in halo_rows(pair):
                copy.start()

        return carry

    lax.fori_loop(0, MESSAGES + LAG, tick, 0)

    for step in range(8):
        copy = momenta_copy(3, step)
        copy.wait() if step == 0 else copy.wait_recv()
        copy = flag_copy(step)
        copy.wait() if step == 0 else copy.wait_recv()
    for pair in range(3):
        for copy in zm_copies(pair):
            copy.wait()
        for copy in tuple(own_rows(pair)) + tuple(halo_rows(pair)):
            copy.wait_recv()
    for copy in z_copies(3) + tuple(own_rows(3)):
        copy.wait_recv()

    phis = (phi0, phi1, phi2, phi3)

    def edge_copies(k, s):
        planes = pl.ds(k + 1, 14 - 2 * k)
        ref = phis[k]
        return (
            remote(ref.at[s, planes, first], ref.at[s, planes, high], d_ss.at[k, s, 0], d_rs.at[k, s, 0], ring(-1)),
            remote(ref.at[s, planes, last], ref.at[s, planes, low], d_ss.at[k, s, 1], d_rs.at[k, s, 1], ring(1)),
        )

    def result_copy(s, h):
        return remote(done.at[s, pl.ds(4 * h, 4)], out.at[0, :, rows_of(q)], e_ss.at[s, h], e_rs.at[q], place(4 * h + s, y, z))

    def result_here(s, h):
        return pltpu.make_async_copy(done.at[s, pl.ds(4 * h, 4)], out.at[0, :, rows_of(q)], here)

    for k in range(1, STEPS + 1):
        for s in ORDER:
            if k > 1:
                for copy in edge_copies(k - 1, s):
                    copy.wait_recv()
            phi = phis[k - 1]
            if k == STEPS:
                tile = flags[s] == 1
                taken = jnp.concatenate([tile] * (ROWS // 8), axis=0)

            def plane_step(plane, carry):
                centre = phi[s, plane, inner, :]
                beside = phi[s, plane - 1, inner, :] + phi[s, plane + 1, inner, :]
                beside = beside + phi[s, plane, pl.ds(PAD - 1, ROWS), :] + phi[s, plane, pl.ds(PAD + 1, ROWS), :]
                beside = beside + pltpu.roll(centre, 1, 1) + pltpu.roll(centre, LANES - 1, 1)
                force = 2.0 * KAPPA * beside - 2.0 * centre - 4.0 * LAMBDA * centre * (centre * centre - 1.0)
                moved = mom[s, plane] + (0.5 * EPS if k == 1 else EPS) * force
                value = centre + EPS * moved
                if k < STEPS:
                    mom[s, plane] = moved
                    phis[k][s, plane, inner, :] = value
                else:
                    done[s, plane - 4] = jnp.where(taken, value, phi0[s, plane, inner, :])
                return carry

            lax.fori_loop(k, 16 - k, plane_step, 0)
            if k < STEPS:
                for copy in edge_copies(k, s):
                    copy.start()
            else:
                for h in range(2):
                    @pl.when(q == 4 * h + s)
                    def _():
                        result_here(s, h).start()

                    @pl.when(q != 4 * h + s)
                    def _():
                        result_copy(s, h).start()

    for pair in range(PAIRS):
        for step in range(1, 8):
            field_copy(pair, step).wait_send()
            momenta_copy(pair, step).wait_send()
        for copy in z_copies(pair) + tuple(own_rows(pair)):
            copy.wait_send()
    for step in range(1, 8):
        flag_copy(step).wait_send()
    for pair in range(3):
        for copy in halo_rows(pair):
            copy.wait_send()

    def left(t, carry):
        up_copy(t).wait_send()
        down_copy(t).wait_send()
        return carry

    lax.fori_loop(0, MESSAGES, left, 0)
    for k in range(1, STEPS):
        for s in range(SLOTS):
            for copy in edge_copies(k, s):
                copy.wait_send()
    for s in range(SLOTS):
        for h in range(2):
            @pl.when(q == 4 * h + s)
            def _():
                result_here(s, h).wait()

            @pl.when(q != 4 * h + s)
            def _():
                result_copy(s, h).wait_send()
    for step in range(1, 8):
        origin = (q + 8 - step) % 8
        remote(done.at[0, pl.ds(0, 4)], out.at[0, :, rows_of(origin)], e_ss.at[0, 0], e_rs.at[origin], ring(step)).wait_recv()


def local(field, momenta, counts, accept):
    f32, dma = jnp.float32, pltpu.SemaphoreType.DMA
    message = (MESSAGES, 4, 2, 8, LANES)
    return pl.pallas_call(
        kernel,
        out_shape=jax.ShapeDtypeStruct(field.shape, f32),
        in_specs=[
            pl.BlockSpec(memory_space=pl.ANY),
            pl.BlockSpec(memory_space=pl.ANY),
            pl.BlockSpec(memory_space=pltpu.SMEM),
            pl.BlockSpec(memory_space=pltpu.SMEM),
        ],
        out_specs=pl.BlockSpec(memory_space=pltpu.VMEM),
        scratch_shapes=[
            pltpu.VMEM((PAIRS, 2, SLOTS, ROWS, LANES), f32),
            pltpu.VMEM(message, f32),
            pltpu.VMEM(message, f32),
            pltpu.VMEM(message, f32),
            pltpu.VMEM(message, f32),
            pltpu.VMEM((SLOTS, 16, ALL, LANES), f32),
            pltpu.VMEM((SLOTS, 16, ALL, LANES), f32),
            pltpu.VMEM((SLOTS, 16, ALL, LANES), f32),
            pltpu.VMEM((SLOTS, 16, ALL, LANES), f32),
            pltpu.VMEM((SLOTS, 16, ROWS, LANES), f32),
            pltpu.VMEM((SLOTS, 8, ROWS, LANES), f32),
            pltpu.VMEM((8, LANES), jnp.int32),
            pltpu.VMEM((8, 8, LANES), jnp.int32),
            dma((PAIRS, 8)), dma((PAIRS, 8)), dma((PAIRS, 8)), dma((PAIRS, 8)), dma((8,)), dma((8,)),
            dma((MESSAGES,)), dma((MESSAGES,)), dma((MESSAGES,)), dma((MESSAGES,)),
            dma((PAIRS, 2)), dma((PAIRS, 2)), dma((3, 2)), dma((3, 2)),
            dma((PAIRS, 2, 2)), dma((PAIRS, 2, 2)), dma((3, 2, 2)), dma((3, 2, 2)),
            dma((STEPS, SLOTS, 2)), dma((STEPS, SLOTS, 2)), dma((SLOTS, 2)), dma((8,)), dma,
        ],
        compiler_params=pltpu.CompilerParams(collective_id=0, has_side_effects=True, vmem_limit_bytes=48 * 1024 * 1024),
    )(field, momenta, counts, accept)


def solution(mesh):
    placed = (P("rep", "gz", None, None), P("rep", "gz", None, None), P(), P("rep"))
    return jax.shard_map(
        local, mesh=mesh, in_specs=placed, out_specs=P("rep", "gz", None, None), check_vma=False
    )
```

```python
import jax
import jax.numpy as jnp
from jax import lax
from jax.experimental import pallas as pl
from jax.experimental.pallas import tpu as pltpu
from jax.sharding import PartitionSpec as P

STEPS = 4
KAPPA = 0.16
LAMBDA = 0.015
EPS = 0.75

MESH = pl.DeviceIdType.MESH
SLOTS = 4
ROWS = 32
PAD = 4
ALL = ROWS + 2 * PAD
LANES = 256
PAIRS = 4
CHUNKS = 16
LAG = 3
MESSAGES = CHUNKS + LAG
ORDER = (0, 2, 1, 3)


def kernel(field, momenta, counts, accept, out, own, send_up, send_down, from_below, from_above, phi0, phi1, phi2, mom,
           done, slab, edges, flag, flags, a_ss, a_rs, c_ss, c_rs, ch_ss, ch_rs, f_ss, f_rs, up_ss, up_rs, down_ss, down_rs, z_ss, z_rs, zm_ss, zm_rs,
           r_ss, r_rs, e_ss, e_rs, here):
    rep, gz = lax.axis_index("rep"), lax.axis_index("gz")
    y, z = rep // 4, gz // 2
    q = (gz % 2) * 4 + rep % 4
    slot, half = rep % 4, gz % 2

    inner = pl.ds(0, ROWS)
    first, last = pl.ds(0, PAD), pl.ds(ROWS - PAD, PAD)
    high, low = pl.ds(ROWS, PAD), pl.ds(ROWS + PAD, PAD)
    beside_inner = pl.ds(ROWS, 2 * PAD)

    def place(ring, row, depth):
        return (row * 4 + ring % 4, depth * 2 + ring // 4)

    def ring(step):
        return place((q + step + 8) % 8, y, z)

    above, below = place(q, (y + 1) % 4, z), place(q, (y + 3) % 4, z)
    z_next, z_last = place(q, y, (z + 1) % 8), place(q, y, (z + 7) % 8)

    def remote(src, dst, ss, rs, device):
        return pltpu.make_async_remote_copy(src_ref=src, dst_ref=dst, send_sem=ss, recv_sem=rs, device_id=device, device_id_type=MESH)

    barrier = pltpu.get_barrier_semaphore()
    partners = [ring(step) for step in range(1, 8)] + [above, below, z_next, z_last]
    for device in partners:
        pl.semaphore_signal(barrier, inc=1, device_id=device, device_id_type=MESH)
    pl.semaphore_wait(barrier, len(partners))

    def rows_of(place_):
        return pl.ds(pl.multiple_of(place_ * ROWS, ROWS), ROWS)

    def local_plane(pair):
        return pair + half * (3 - 2 * pair)

    def field_copy(pair, step):
        src = field.at[0, local_plane(pair), rows_of((q + step) % 8)]
        dst = own.at[pair, half, slot]
        if step == 0:
            return pltpu.make_async_copy(src, dst, a_rs.at[pair, 0])
        return remote(src, dst, a_ss.at[pair, step], a_rs.at[pair, step], ring(step))

    def momenta_copy(pair, step):
        src = momenta.at[0, local_plane(pair), rows_of((q + step) % 8)]
        dst = mom.at[slot, 4 + half * 4 + local_plane(pair), inner]
        if step == 0:
            return pltpu.make_async_copy(src, dst, c_rs.at[pair, 0])
        return remote(src, dst, c_ss.at[pair, step], c_rs.at[pair, step], ring(step))

    def edge_copy(step):
        src, dst = edges.at[step], mom.at[slot, pl.ds(4 + half * 4, 4), beside_inner]
        if step == 0:
            return pltpu.make_async_copy(src, dst, ch_rs.at[0])
        return remote(src, dst, ch_ss.at[step], ch_rs.at[step], ring(step))

    whole_momenta = pltpu.make_async_copy(momenta.at[0], slab, here)
    whole_momenta.start()

    def fill_edges():
        upper = lax.broadcasted_iota(jnp.int32, (8, LANES), 0) < PAD
        for step in range(8):
            base = ((q + step) % 8) * ROWS
            after = pl.ds(pl.multiple_of((base + ROWS) % 256, 8), 8)
            ahead = pl.ds(pl.multiple_of((base + 248) % 256, 8), 8)
            for plane in range(4):
                edges[step, plane] = jnp.where(upper, slab[plane, after, :], slab[plane, ahead, :])

    def flag_copy(step):
        if step == 0:
            return pltpu.make_async_copy(flag, flags.at[q], f_rs.at[0])
        return remote(flag, flags.at[q], f_ss.at[step], f_rs.at[step], ring(step))

    for step in range(8):
        field_copy(0, step).start()
    flag[...] = jnp.full(flag.shape, accept[0], jnp.int32)
    for step in range(8):
        flag_copy(step).start()

    alive = [[(counts[4 * ((y + d) % 4) + i] > 0).astype(jnp.int32) for i in range(4)] for d in range(4)]
    before = [[sum(alive[d][:i], jnp.int32(0)) for i in range(4)] for d in range(4)]
    total = [sum(alive[d], jnp.int32(0)) for d in range(4)]
    mine = [jnp.int32(-1)] * 4
    for c in range(4):
        for i in range(4):
            mine[c] = jnp.where((alive[0][i] == 1) & (before[0][i] == c), i, mine[c])
    split_up = jnp.minimum(total[3], 4 - total[2])
    split = jnp.minimum(total[2], 4 - total[1])
    cum, parent = jnp.int32(0), [jnp.int32(0)] * SLOTS
    for r in range(16):
        cum = cum + counts[r]
        for s in range(SLOTS):
            parent[s] = parent[s] + (cum <= 4 * y + s).astype(jnp.int32)
    code = []
    for s in range(SLOTS):
        value = jnp.int32(0)
        for d in range(4):
            for i in range(4):
                k = before[d][i]
                if d == 0:
                    way = jnp.int32(i)
                elif d == 1:
                    way = 4 + k
                elif d == 3:
                    way = 8 + k
                else:
                    way = jnp.where(k < split, 12 + total[1] + k, 16 + total[3] + k - split)
                value = jnp.where(parent[s] == 4 * ((y + d) % 4) + i, way, value)
        code.append(value)

    def same(value, number):
        return jnp.full((8, LANES), value, jnp.int32) == number

    def octet(t):
        return t // 4, pl.ds(pl.multiple_of((t % 4) * 8, 8), 8)

    def assemble(t, forward):
        pair, rows = octet(jnp.minimum(t, CHUNKS - 1))
        for c in range(4):
            own_here = [same(mine[c], i) for i in range(4)]
            down_here = [same(total[0], c - f) for f in range(c + 1)]
            up_here = [same(split_up + c - total[0], f) for f in range(4)]
            for h in range(2):
                pieces = [own[pair, h, i, rows, :] for i in range(4)]
                if forward:
                    down, up = from_above[t - LAG, 0, h], from_below[t - LAG, 0, h]
                    for f in range(1, c + 1):
                        down = jnp.where(down_here[f], from_above[t - LAG, f, h], down)
                    for f in range(1, 4):
                        up = jnp.where(up_here[f], from_below[t - LAG, f, h], up)
                else:
                    down = up = pieces[0]
                for i in range(4):
                    down = jnp.where(own_here[i], pieces[i], down)
                    up = jnp.where(own_here[i], pieces[i], up)
                send_down[t, c, h] = down
                send_up[t, c, h] = up

    def up_copy(t):
        return remote(send_up.at[t], from_below.at[t], up_ss.at[t], up_rs.at[t], above)

    def down_copy(t):
        return remote(send_down.at[t], from_above.at[t], down_ss.at[t], down_rs.at[t], below)

    def pick(u):
        pair, rows = octet(u)
        for s in range(SLOTS):
            here_ = [same(code[s], k) for k in range(20)]
            for h in range(2):
                value = own[pair, h, 0, rows, :]
                for i in range(1, 4):
                    value = jnp.where(here_[i], own[pair, h, i, rows, :], value)
                for c in range(4):
                    value = jnp.where(here_[4 + c], from_above[u, c, h], value)
                    value = jnp.where(here_[8 + c], from_below[u, c, h], value)
                    value = jnp.where(here_[12 + c], from_above[u + LAG, c, h], value)
                    value = jnp.where(here_[16 + c], from_below[u + LAG, c, h], value)
                plane = 4 + pair if h == 0 else 11 - pair
                phi0[s, plane, rows, :] = value

    def z_copies(pair, rows):
        return (
            remote(phi0.at[:, 4 + pair, rows], phi0.at[:, 12 + pair, rows], z_ss.at[pair, 0], z_rs.at[pair, 0], z_last),
            remote(phi0.at[:, 11 - pair, rows], phi0.at[:, 3 - pair, rows], z_ss.at[pair, 1], z_rs.at[pair, 1], z_next),
        )

    def zm_copies(pair):
        return (
            remote(mom.at[:, 4 + pair], mom.at[:, 12 + pair], zm_ss.at[pair, 0], zm_rs.at[pair, 0], z_last),
            remote(mom.at[:, 11 - pair], mom.at[:, 3 - pair], zm_ss.at[pair, 1], zm_rs.at[pair, 1], z_next),
        )

    def row_copies(pair):
        copies = []
        for n, plane in enumerate((4 + pair, 11 - pair)):
            copies.append(remote(phi0.at[:, plane, first], phi0.at[:, plane, high], r_ss.at[pair, n, 0], r_rs.at[pair, n, 0], ring(-1)))
            copies.append(remote(phi0.at[:, plane, last], phi0.at[:, plane, low], r_ss.at[pair, n, 1], r_rs.at[pair, n, 1], ring(1)))
        return copies

    whole = pl.ds(0, ALL)

    def tick(t, carry):
        @pl.when((t < 6) & (t % 2 == 0))
        def _():
            for step in range(1, 8):
                field_copy(t // 2, step).wait_send()
            for step in range(8):
                field_copy(t // 2 + 1, step).start()

        @pl.when((t % 4 == 0) & (t < CHUNKS))
        def _():
            for step in range(8):
                copy = field_copy(t // 4, step)
                copy.wait() if step == 0 else copy.wait_recv()

        @pl.when(t >= LAG)
        def _():
            up_copy(t - LAG).wait_recv()
            down_copy(t - LAG).wait_recv()

        @pl.when(t < LAG)
        def _():
            assemble(t, False)

        @pl.when((t >= LAG) & (t < MESSAGES))
        def _():
            assemble(t, True)

        @pl.when(t < MESSAGES)
        def _():
            up_copy(t).start()
            down_copy(t).start()

        @pl.when(t == 6)
        def _():
            whole_momenta.wait()
            fill_edges()
            for step in range(8):
                edge_copy(step).start()

        @pl.when((t >= 6) & (t < 14) & (t % 2 == 0))
        def _():
            for step in range(8):
                momenta_copy((t - 6) // 2, step).start()

        @pl.when(t >= 2 * LAG)
        def _():
            pick(t - 2 * LAG)

        @pl.when((t >= 2 * LAG + 3) & ((t - 2 * LAG) % 4 == 3))
        def _():
            for copy in row_copies((t - 2 * LAG - 3) // 4):
                copy.start()

        @pl.when((t >= 2 * LAG + 5) & ((t - 2 * LAG) % 4 == 1))
        def _():
            pair = (t - 2 * LAG - 5) // 4
            for copy in row_copies(pair):
                copy.wait_recv()
            for copy in z_copies(pair, whole):
                copy.start()

        @pl.when(t == 12)
        def _():
            for step in range(8):
                copy = edge_copy(step)
                copy.wait() if step == 0 else copy.wait_recv()

        @pl.when((t == 12) | (t == 14) | (t == 16))
        def _():
            pair = (t - 12) // 2
            for step in range(8):
                copy = momenta_copy(pair, step)
                copy.wait() if step == 0 else copy.wait_recv()
            for copy in zm_copies(pair):
                copy.start()

        return carry

    lax.fori_loop(0, MESSAGES + LAG, tick, 0)

    for copy in z_copies(3, inner):
        copy.start()
    for step in range(8):
        copy = momenta_copy(3, step)
        copy.wait() if step == 0 else copy.wait_recv()
        copy = flag_copy(step)
        copy.wait() if step == 0 else copy.wait_recv()
    for pair in range(3):
        for copy in zm_copies(pair):
            copy.wait()
        for copy in z_copies(pair, whole):
            copy.wait_recv()
    for copy in z_copies(3, inner) + tuple(row_copies(3)):
        copy.wait_recv()

    def result_copy(s, h):
        return remote(done.at[s, pl.ds(4 * h, 4)], out.at[0, :, rows_of(q)], e_ss.at[s, h], e_rs.at[q], place(4 * h + s, y, z))

    def result_here(s, h):
        return pltpu.make_async_copy(done.at[s, pl.ds(4 * h, 4)], out.at[0, :, rows_of(q)], here)

    def force(centre, beside):
        beside = beside + pltpu.roll(centre, 1, 0) + pltpu.roll(centre, ALL - 1, 0)
        beside = beside + pltpu.roll(centre, 1, 1) + pltpu.roll(centre, LANES - 1, 1)
        return 2.0 * KAPPA * beside - 2.0 * centre - 4.0 * LAMBDA * centre * (centre * centre - 1.0)

    for s in ORDER:
        steps = (phi0.at[s], phi1, phi2, phi1)
        taken = jnp.concatenate([flags[s] == 1] * (ROWS // 8), axis=0)
        for k in range(1, STEPS + 1):
            phi = steps[k - 1]

            def plane_step(plane, carry):
                centre = phi[plane]
                moved = mom[s, plane] + (0.5 * EPS if k == 1 else EPS) * force(centre, phi[plane - 1] + phi[plane + 1])
                value = centre + EPS * moved
                if k < STEPS:
                    mom[s, plane] = moved
                    steps[k][plane] = value
                else:
                    done[s, plane - 4] = jnp.where(taken, value[:ROWS], phi0[s, plane, inner, :])
                return carry

            lax.fori_loop(k, 16 - k, plane_step, 0, unroll=2)
        for h in range(2):
            @pl.when(q == 4 * h + s)
            def _():
                result_here(s, h).start()

            @pl.when(q != 4 * h + s)
            def _():
                result_copy(s, h).start()

    for pair in range(PAIRS):
        for step in range(1, 8):
            momenta_copy(pair, step).wait_send()
        for copy in z_copies(pair, whole if pair < 3 else inner) + tuple(row_copies(pair)):
            copy.wait_send()
    for step in range(1, 8):
        flag_copy(step).wait_send()
        field_copy(3, step).wait_send()
        edge_copy(step).wait_send()

    def left(t, carry):
        up_copy(t).wait_send()
        down_copy(t).wait_send()
        return carry

    lax.fori_loop(0, MESSAGES, left, 0)
    for s in range(SLOTS):
        for h in range(2):
            @pl.when(q == 4 * h + s)
            def _():
                result_here(s, h).wait()

            @pl.when(q != 4 * h + s)
            def _():
                result_copy(s, h).wait_send()
    for step in range(1, 8):
        origin = (q + 8 - step) % 8
        remote(done.at[0, pl.ds(0, 4)], out.at[0, :, rows_of(origin)], e_ss.at[0, 0], e_rs.at[origin], ring(step)).wait_recv()


def local(field, momenta, counts, accept):
    f32, dma = jnp.float32, pltpu.SemaphoreType.DMA
    message = (MESSAGES, 4, 2, 8, LANES)
    return pl.pallas_call(
        kernel,
        out_shape=jax.ShapeDtypeStruct(field.shape, f32),
        in_specs=[
            pl.BlockSpec(memory_space=pltpu.HBM),
            pl.BlockSpec(memory_space=pltpu.HBM),
            pl.BlockSpec(memory_space=pltpu.SMEM),
            pl.BlockSpec(memory_space=pltpu.SMEM),
        ],
        out_specs=pl.BlockSpec(memory_space=pl.ANY),
        scratch_shapes=[
            pltpu.VMEM((PAIRS, 2, SLOTS, ROWS, LANES), f32),
            pltpu.VMEM(message, f32),
            pltpu.VMEM(message, f32),
            pltpu.VMEM(message, f32),
            pltpu.VMEM(message, f32),
            pltpu.VMEM((SLOTS, 16, ALL, LANES), f32),
            pltpu.VMEM((16, ALL, LANES), f32),
            pltpu.VMEM((16, ALL, LANES), f32),
            pltpu.VMEM((SLOTS, 16, ALL, LANES), f32),
            pltpu.VMEM((SLOTS, 8, ROWS, LANES), f32),
            pltpu.VMEM((4, 256, LANES), f32),
            pltpu.VMEM((8, 4, 8, LANES), f32),
            pltpu.VMEM((8, LANES), jnp.int32),
            pltpu.VMEM((8, 8, LANES), jnp.int32),
            dma((PAIRS, 8)), dma((PAIRS, 8)), dma((PAIRS, 8)), dma((PAIRS, 8)), dma((8,)), dma((8,)), dma((8,)), dma((8,)),
            dma((MESSAGES,)), dma((MESSAGES,)), dma((MESSAGES,)), dma((MESSAGES,)),
            dma((PAIRS, 2)), dma((PAIRS, 2)), dma((3, 2)), dma((3, 2)),
            dma((PAIRS, 2, 2)), dma((PAIRS, 2, 2)), dma((SLOTS, 2)), dma((8,)), dma,
        ],
        compiler_params=pltpu.CompilerParams(collective_id=0, has_side_effects=True, vmem_limit_bytes=60 * 1024 * 1024),
    )(field, momenta, counts, accept)


def solution(mesh):
    placed = (P("rep", "gz", None, None), P("rep", "gz", None, None), P(), P("rep"))
    return jax.shard_map(
        local, mesh=mesh, in_specs=placed, out_specs=P("rep", "gz", None, None), check_vma=False
    )
```

```python
import jax
import jax.numpy as jnp
from jax import lax
from jax.experimental import pallas as pl
from jax.experimental.pallas import tpu as pltpu
from jax.sharding import PartitionSpec as P

KAPPA = 0.16
LAMBDA = 0.015
EPS = 0.75

MESH = pl.DeviceIdType.MESH
SLOTS = 4
ROWS = 32
PAD = 4
ALL = ROWS + 2 * PAD
SIDE = 256
LANES = 128
PAIRS = 4
CHUNKS = 16
LAG = 3
MESSAGES = CHUNKS + LAG


def kernel(field, momenta, counts, accept, out, own, send_up, send_down, from_below, from_above, phi0, phi1, phi2, phi3, mom, moves, moves_at_ends, sides,
           done, turned, fields, slab, edges, flag, flags, a_ss, a_rs, c_ss, c_rs, ch_ss, ch_rs, f_ss, f_rs, up_ss, up_rs, down_ss, down_rs, z_ss, z_rs, zm_ss, zm_rs,
           r_ss, r_rs, d_ss, d_rs, e_ss, e_rs, here, home):
    rep, gz = lax.axis_index("rep"), lax.axis_index("gz")
    y, z = rep // 4, gz // 2
    q = (gz % 2) * 4 + rep % 4
    slot, half = rep % 4, gz % 2

    inner = pl.ds(0, ROWS)
    first, last = pl.ds(0, PAD), pl.ds(ROWS - PAD, PAD)
    high, low = pl.ds(ROWS, PAD), pl.ds(ROWS + PAD, PAD)
    beside_inner = pl.ds(ROWS, 2 * PAD)

    def place(ring, row, depth):
        return (row * 4 + ring % 4, depth * 2 + ring // 4)

    def ring(step):
        return place((q + step + 8) % 8, y, z)

    above, below = place(q, (y + 1) % 4, z), place(q, (y + 3) % 4, z)
    z_next, z_last = place(q, y, (z + 1) % 8), place(q, y, (z + 7) % 8)

    def remote(src, dst, ss, rs, device):
        return pltpu.make_async_remote_copy(src_ref=src, dst_ref=dst, send_sem=ss, recv_sem=rs, device_id=device, device_id_type=MESH)

    loads = [[], []]
    for n, (src, dst) in enumerate(((field, fields), (momenta, slab))):
        for side in range(2):
            loads[n].append(pltpu.make_async_copy(src.at[0, :, :, pl.ds(side * LANES, LANES)], dst.at[:, side], here.at[n, side]))
            loads[n][side].start()

    barrier = pltpu.get_barrier_semaphore()
    partners = [ring(step) for step in range(1, 8)] + [above, below, z_next, z_last]
    for device in partners:
        pl.semaphore_signal(barrier, inc=1, device_id=device, device_id_type=MESH)
    pl.semaphore_wait(barrier, len(partners))

    def rows_of(place_):
        return pl.ds(pl.multiple_of(place_ * ROWS, ROWS), ROWS)

    def local_plane(pair):
        return pair + half * (3 - 2 * pair)

    def field_copy(pair, step):
        src = fields.at[local_plane(pair), :, rows_of((q + step) % 8)]
        dst = own.at[pair, half, slot]
        if step == 0:
            return pltpu.make_async_copy(src, dst, a_rs.at[pair, 0])
        return remote(src, dst, a_ss.at[pair, step], a_rs.at[pair, step], ring(step))

    def momenta_copy(pair, step):
        src = slab.at[local_plane(pair), :, rows_of((q + step) % 8)]
        dst = mom.at[slot, 4 + half * 4 + local_plane(pair), :, inner]
        if step == 0:
            return pltpu.make_async_copy(src, dst, c_rs.at[pair, 0])
        return remote(src, dst, c_ss.at[pair, step], c_rs.at[pair, step], ring(step))

    def edge_copy(step):
        src, dst = edges.at[step], mom.at[slot, pl.ds(4 + half * 4, 4), :, beside_inner]
        if step == 0:
            return pltpu.make_async_copy(src, dst, ch_rs.at[0])
        return remote(src, dst, ch_ss.at[step], ch_rs.at[step], ring(step))

    def fill_edges():
        upper = lax.broadcasted_iota(jnp.int32, (2, 8, LANES), 1) < PAD
        for step in range(8):
            base = ((q + step) % 8) * ROWS
            after = pl.ds(pl.multiple_of((base + ROWS) % SIDE, 8), 8)
            ahead = pl.ds(pl.multiple_of((base + SIDE - 8) % SIDE, 8), 8)
            for plane in range(4):
                edges[step, plane] = jnp.where(upper, slab[plane, :, after, :], slab[plane, :, ahead, :])

    def flag_copy(step):
        if step == 0:
            return pltpu.make_async_copy(flag, flags.at[q], f_rs.at[0])
        return remote(flag, flags.at[q], f_ss.at[step], f_rs.at[step], ring(step))

    for load in loads[0]:
        load.wait()
    for step in range(8):
        field_copy(0, step).start()
    flag[...] = jnp.full(flag.shape, accept[0], jnp.int32)
    for step in range(8):
        flag_copy(step).start()

    alive = [[(counts[4 * ((y + d) % 4) + i] > 0).astype(jnp.int32) for i in range(4)] for d in range(4)]
    before = [[sum(alive[d][:i], jnp.int32(0)) for i in range(4)] for d in range(4)]
    total = [sum(alive[d], jnp.int32(0)) for d in range(4)]
    mine = [jnp.int32(-1)] * 4
    for c in range(4):
        for i in range(4):
            mine[c] = jnp.where((alive[0][i] == 1) & (before[0][i] == c), i, mine[c])
    split_up = jnp.minimum(total[3], 4 - total[2])
    split = jnp.minimum(total[2], 4 - total[1])
    cum, parent = jnp.int32(0), [jnp.int32(0)] * SLOTS
    for r in range(16):
        cum = cum + counts[r]
        for s in range(SLOTS):
            parent[s] = parent[s] + (cum <= 4 * y + s).astype(jnp.int32)
    code = []
    for s in range(SLOTS):
        value = jnp.int32(0)
        for d in range(4):
            for i in range(4):
                k = before[d][i]
                if d == 0:
                    way = jnp.int32(i)
                elif d == 1:
                    way = 4 + k
                elif d == 3:
                    way = 8 + k
                else:
                    way = jnp.where(k < split, 12 + total[1] + k, 16 + total[3] + k - split)
                value = jnp.where(parent[s] == 4 * ((y + d) % 4) + i, way, value)
        code.append(value)

    def same(value, number):
        return jnp.full((2, 8, LANES), value, jnp.int32) == number

    def octet(t):
        return t // 4, pl.ds(pl.multiple_of((t % 4) * 8, 8), 8)

    def assemble(t, forward):
        pair, rows = octet(jnp.minimum(t, CHUNKS - 1))
        for c in range(4):
            own_here = [same(mine[c], i) for i in range(4)]
            down_here = [same(total[0], c - f) for f in range(c + 1)]
            up_here = [same(split_up + c - total[0], f) for f in range(4)]
            for h in range(2):
                pieces = [own[pair, h, i, :, rows, :] for i in range(4)]
                if forward:
                    down, up = from_above[t - LAG, 0, h], from_below[t - LAG, 0, h]
                    for f in range(1, c + 1):
                        down = jnp.where(down_here[f], from_above[t - LAG, f, h], down)
                    for f in range(1, 4):
                        up = jnp.where(up_here[f], from_below[t - LAG, f, h], up)
                else:
                    down = up = pieces[0]
                for i in range(4):
                    down = jnp.where(own_here[i], pieces[i], down)
                    up = jnp.where(own_here[i], pieces[i], up)
                send_down[t, c, h] = down
                send_up[t, c, h] = up

    def up_copy(t):
        return remote(send_up.at[t], from_below.at[t], up_ss.at[t], up_rs.at[t], above)

    def down_copy(t):
        return remote(send_down.at[t], from_above.at[t], down_ss.at[t], down_rs.at[t], below)

    def pick(u):
        pair, rows = octet(u)
        for s in range(SLOTS):
            here_ = [same(code[s], k) for k in range(20)]
            for h in range(2):
                value = own[pair, h, 0, :, rows, :]
                for i in range(1, 4):
                    value = jnp.where(here_[i], own[pair, h, i, :, rows, :], value)
                for c in range(4):
                    value = jnp.where(here_[4 + c], from_above[u, c, h], value)
                    value = jnp.where(here_[8 + c], from_below[u, c, h], value)
                    value = jnp.where(here_[12 + c], from_above[u + LAG, c, h], value)
                    value = jnp.where(here_[16 + c], from_below[u + LAG, c, h], value)
                plane = 4 + pair if h == 0 else 11 - pair
                phi0[s, plane, :, rows, :] = value

    def z_copies(pair):
        return (
            remote(phi0.at[:, 4 + pair], phi0.at[:, 12 + pair], z_ss.at[pair, 0], z_rs.at[pair, 0], z_last),
            remote(phi0.at[:, 11 - pair], phi0.at[:, 3 - pair], z_ss.at[pair, 1], z_rs.at[pair, 1], z_next),
        )

    def zm_copies(pair):
        return (
            remote(mom.at[:, 4 + pair], mom.at[:, 12 + pair], zm_ss.at[pair, 0], zm_rs.at[pair, 0], z_last),
            remote(mom.at[:, 11 - pair], mom.at[:, 3 - pair], zm_ss.at[pair, 1], zm_rs.at[pair, 1], z_next),
        )

    def row_copies(pair):
        copies = []
        for n, plane in enumerate((4 + pair, 11 - pair)):
            copies.append(remote(phi0.at[:, plane, :, first], phi0.at[:, plane, :, high], r_ss.at[pair, n, 0], r_rs.at[pair, n, 0], ring(-1)))
            copies.append(remote(phi0.at[:, plane, :, last], phi0.at[:, plane, :, low], r_ss.at[pair, n, 1], r_rs.at[pair, n, 1], ring(1)))
        return copies

    def tick(t, carry):
        @pl.when(t < 3)
        def _():
            for step in range(8):
                field_copy(t + 1, step).start()

        @pl.when((t % 4 == 0) & (t < CHUNKS))
        def _():
            for step in range(8):
                copy = field_copy(t // 4, step)
                copy.wait() if step == 0 else copy.wait_recv()

        @pl.when(t >= LAG)
        def _():
            up_copy(t - LAG).wait_recv()
            down_copy(t - LAG).wait_recv()

        @pl.when(t < LAG)
        def _():
            assemble(t, False)

        @pl.when((t >= LAG) & (t < MESSAGES))
        def _():
            assemble(t, True)

        @pl.when(t < MESSAGES)
        def _():
            up_copy(t).start()
            down_copy(t).start()

        @pl.when(t == 4)
        def _():
            for load in loads[1]:
                load.wait()
            fill_edges()
            for step in range(8):
                edge_copy(step).start()

        @pl.when((t >= 6) & (t < 14) & (t % 2 == 0))
        def _():
            for step in range(8):
                momenta_copy((t - 6) // 2, step).start()

        @pl.when(t >= 2 * LAG)
        def _():
            pick(t - 2 * LAG)

        @pl.when((t >= 2 * LAG + 3) & ((t - 2 * LAG) % 4 == 3))
        def _():
            for copy in row_copies((t - 2 * LAG - 3) // 4):
                copy.start()

        @pl.when((t == 2 * LAG + 5) | (t == 2 * LAG + 9) | (t == 2 * LAG + 13))
        def _():
            pair = (t - 2 * LAG - 5) // 4
            for copy in row_copies(pair):
                copy.wait_recv()
            for copy in z_copies(pair):
                copy.start()

        @pl.when(t == 12)
        def _():
            for step in range(8):
                copy = edge_copy(step)
                copy.wait() if step == 0 else copy.wait_recv()

        @pl.when((t == 12) | (t == 14))
        def _():
            pair = (t - 12) // 2
            for step in range(8):
                copy = momenta_copy(pair, step)
                copy.wait() if step == 0 else copy.wait_recv()
            for copy in zm_copies(pair):
                copy.start()

        return carry

    lax.fori_loop(0, MESSAGES + LAG, tick, 0)

    for pair in range(2, PAIRS):
        for step in range(8):
            copy = momenta_copy(pair, step)
            copy.wait() if step == 0 else copy.wait_recv()
    for step in range(8):
        copy = flag_copy(step)
        copy.wait() if step == 0 else copy.wait_recv()
    for pair in range(2):
        for copy in zm_copies(pair):
            copy.wait()
    for pair in range(3):
        for copy in z_copies(pair):
            copy.wait_recv()
    for copy in row_copies(3):
        copy.wait_recv()

    def last_copies(s):
        return (
            remote(phi3.at[s, 0], sides.at[s, 1], d_ss.at[s, 0], d_rs.at[s, 0], z_last),
            remote(phi3.at[s, 7], sides.at[s, 0], d_ss.at[s, 1], d_rs.at[s, 1], z_next),
        )

    def result_copy(s, h, part, away):
        if part == 0:
            here_, there = pl.ds(1 + 3 * h, 3), pl.ds(1 - h, 3)
        else:
            here_, there = pl.ds(7 * h, 1), pl.ds(3 * h, 1)
        src, dst = done.at[s, here_], out.at[0, there, rows_of(q)]
        if away:
            return remote(src, dst, e_ss.at[s, h, part], e_rs.at[part, q], place(4 * h + s, y, z))
        return pltpu.make_async_copy(src, dst, home.at[part])

    def results(s, part, act):
        for h in range(2):
            @pl.when(q == 4 * h + s)
            def _():
                act(result_copy(s, h, part, False), False)

            @pl.when(q != 4 * h + s)
            def _():
                act(result_copy(s, h, part, True), True)

    tiles = range(ALL // 8)

    def spread(t):
        return pl.ds(t, 8, stride=ALL // 8)

    edge_lane = lax.broadcasted_iota(jnp.int32, (8, LANES), 1)
    first_lane, last_lane = edge_lane == 0, edge_lane == LANES - 1

    def natural(ref, plane):
        return [[ref[plane, n, spread(t), :] for t in tiles] for n in range(2)]

    def packed(ref, plane):
        return [[ref[plane, n, 8 * t:8 * t + 8, :] for t in tiles] for n in range(2)]

    def keep(ref, plane, values):
        for n in range(2):
            for t in tiles:
                ref[plane, n, 8 * t:8 * t + 8, :] = values[n][t]

    def each(act, *args):
        return [[act(*(arg[n][t] for arg in args)) for t in tiles] for n in range(2)]

    def kick(below_, centre, above_, scale):
        back = [[pltpu.roll(centre[n][t], 1, 1) for t in tiles] for n in range(2)]
        fore = [[pltpu.roll(centre[n][t], LANES - 1, 1) for t in tiles] for n in range(2)]
        result = [[], []]
        for n in range(2):
            for t in tiles:
                c = centre[n][t]
                ahead = centre[n][t - 1] if t > 0 else pltpu.roll(centre[n][-1], 1, 0)
                after = centre[n][t + 1] if t < len(tiles) - 1 else pltpu.roll(centre[n][0], 7, 0)
                left_ = jnp.where(first_lane, back[1 - n][t], back[n][t])
                right_ = jnp.where(last_lane, fore[1 - n][t], fore[n][t])
                beside = (below_[n][t] + above_[n][t]) + (ahead + after) + (left_ + right_)
                result[n].append((scale * 2.0 * KAPPA) * beside + c * (scale * (4.0 * LAMBDA - 2.0) - (scale * 4.0 * LAMBDA) * (c * c)))
        return result

    def finish(s, taken, plane, trio, move):
        push = kick(*trio, EPS * EPS)
        start = natural(phi0.at[s], 4 + plane)
        value = each(lambda c, m, f, b: jnp.where(taken, c + (m + f), b), trio[1], move, push, start)
        for n in range(2):
            for t in tiles:
                turned[plane, n, spread(t), :] = value[n][t]
            done[s, plane, :, n * LANES:(n + 1) * LANES] = turned[plane, n, :ROWS, :]

    def one_slot(n, carry):
        s = (n % 2) * 2 + n // 2
        taken = flags[s] == 1
        start = phi0.at[s]
        trio = [None, natural(start, 1), natural(start, 2)]
        for plane in range(2, 14):
            trio = trio[1:] + [natural(start, plane + 1)]
            move, push = natural(mom.at[s], plane), kick(*trio, 0.5 * EPS * EPS)
            move = each(lambda m, f: EPS * m + f, move, push)
            keep(moves, plane, move)
            keep(phi1, plane, each(lambda c, m: c + m, trio[1], move))
        for k, source, target in ((2, phi1, phi2), (3, phi2, phi3.at[s])):
            trio = [None, packed(source, k), packed(source, k + 1)]
            for plane in range(k + 1, 15 - k):
                trio = trio[1:] + [packed(source, plane + 1)]
                move, push = packed(moves, plane), kick(*trio, EPS * EPS)
                move = each(lambda m, f: m + f, move, push)
                if k == 3 and plane in (4, 11):
                    keep(moves_at_ends.at[s], plane // 11, move)
                else:
                    keep(moves, plane, move)
                keep(target, plane - (4 if k == 3 else 0), each(lambda c, m: c + m, trio[1], move))
        for copy in last_copies(s):
            copy.start()
        mine_ = phi3.at[s]
        trio = [None, packed(mine_, 0), packed(mine_, 1)]
        for plane in range(1, 7):
            trio = trio[1:] + [packed(mine_, plane + 1)]
            finish(s, taken, plane, trio, packed(moves, 4 + plane))
        results(s, 0, lambda copy, away: copy.start())
        return carry

    def both_ends(n, carry):
        s = (n % 2) * 2 + n // 2
        taken = flags[s] == 1
        for copy in last_copies(s):
            copy.wait_recv()
        mine_, beyond, held = phi3.at[s], sides.at[s], moves_at_ends.at[s]
        finish(s, taken, 0, [packed(beyond, 0), packed(mine_, 0), packed(mine_, 1)], packed(held, 0))
        finish(s, taken, 7, [packed(mine_, 6), packed(mine_, 7), packed(beyond, 1)], packed(held, 1))
        results(s, 1, lambda copy, away: copy.start())
        return carry

    lax.fori_loop(0, SLOTS, one_slot, 0)
    lax.fori_loop(0, SLOTS, both_ends, 0)

    for pair in range(PAIRS):
        for step in range(1, 8):
            field_copy(pair, step).wait_send()
            momenta_copy(pair, step).wait_send()
        for copy in row_copies(pair):
            copy.wait_send()
    for pair in range(3):
        for copy in z_copies(pair):
            copy.wait_send()
    for step in range(1, 8):
        flag_copy(step).wait_send()
        edge_copy(step).wait_send()

    def left(t, carry):
        up_copy(t).wait_send()
        down_copy(t).wait_send()
        return carry

    lax.fori_loop(0, MESSAGES, left, 0)
    for s in range(SLOTS):
        for copy in last_copies(s):
            copy.wait_send()
        for part in range(2):
            results(s, part, lambda copy, away: copy.wait_send() if away else copy.wait())
    for part in range(2):
        for step in range(1, 8):
            origin = (q + 8 - step) % 8
            size = pl.ds(0, 3 if part == 0 else 1)
            remote(done.at[0, size], out.at[0, size, rows_of(origin)], e_ss.at[0, 0, 0], e_rs.at[part, origin], ring(step)).wait_recv()


def local(field, momenta, counts, accept):
    f32, dma = jnp.float32, pltpu.SemaphoreType.DMA
    message = (MESSAGES, 4, 2, 2, 8, LANES)
    plane = (2, ALL, LANES)
    return pl.pallas_call(
        kernel,
        out_shape=jax.ShapeDtypeStruct(field.shape, f32),
        in_specs=[
            pl.BlockSpec(memory_space=pltpu.HBM),
            pl.BlockSpec(memory_space=pltpu.HBM),
            pl.BlockSpec(memory_space=pltpu.SMEM),
            pl.BlockSpec(memory_space=pltpu.SMEM),
        ],
        out_specs=pl.BlockSpec(memory_space=pl.ANY),
        scratch_shapes=[
            pltpu.VMEM((PAIRS, 2, SLOTS, 2, ROWS, LANES), f32),
            pltpu.VMEM(message, f32),
            pltpu.VMEM(message, f32),
            pltpu.VMEM(message, f32),
            pltpu.VMEM(message, f32),
            pltpu.VMEM((SLOTS, 16) + plane, f32),
            pltpu.VMEM((16,) + plane, f32),
            pltpu.VMEM((16,) + plane, f32),
            pltpu.VMEM((SLOTS, 8) + plane, f32),
            pltpu.VMEM((SLOTS, 16) + plane, f32),
            pltpu.VMEM((16,) + plane, f32),
            pltpu.VMEM((SLOTS, 2) + plane, f32),
            pltpu.VMEM((SLOTS, 2) + plane, f32),
            pltpu.VMEM((SLOTS, 8, ROWS, SIDE), f32),
            pltpu.VMEM((8,) + plane, f32),
            pltpu.VMEM((4, 2, SIDE, LANES), f32),
            pltpu.VMEM((4, 2, SIDE, LANES), f32),
            pltpu.VMEM((8, 4, 2, 8, LANES), f32),
            pltpu.VMEM((8, LANES), jnp.int32),
            pltpu.VMEM((8, 8, LANES), jnp.int32),
            dma((PAIRS, 8)), dma((PAIRS, 8)), dma((PAIRS, 8)), dma((PAIRS, 8)), dma((8,)), dma((8,)), dma((8,)), dma((8,)),
            dma((MESSAGES,)), dma((MESSAGES,)), dma((MESSAGES,)), dma((MESSAGES,)),
            dma((3, 2)), dma((3, 2)), dma((2, 2)), dma((2, 2)),
            dma((PAIRS, 2, 2)), dma((PAIRS, 2, 2)), dma((SLOTS, 2)), dma((SLOTS, 2)), dma((SLOTS, 2, 2)), dma((2, 8)), dma((2, 2)), dma((2,)),
        ],
        compiler_params=pltpu.CompilerParams(collective_id=0, has_side_effects=True, vmem_limit_bytes=60 * 1024 * 1024),
    )(field, momenta, counts, accept)


def solution(mesh):
    placed = (P("rep", "gz", None, None), P("rep", "gz", None, None), P(), P("rep"))
    return jax.shard_map(
        local, mesh=mesh, in_specs=placed, out_specs=P("rep", "gz", None, None), check_vma=False
    )
```

```python
import jax
import jax.numpy as jnp
from jax import lax
from jax.experimental import pallas as pl
from jax.experimental.pallas import tpu as pltpu
from jax.sharding import PartitionSpec as P

KAPPA = 0.16
LAMBDA = 0.015
EPS = 0.75

MESH = pl.DeviceIdType.MESH
SLOTS = 4
ROWS = 32
PAD = 4
ALL = ROWS + 2 * PAD
SIDE = 256
LANES = 128
PAIRS = 4
CHUNKS = 16
LAG = 3
MESSAGES = CHUNKS + LAG


def kernel(field, momenta, counts, accept, out, own, send_up, send_down, from_below, from_above, phi0, phi1, phi2, phi3, mom, moves, sides,
           done, turned, fields, slab, edges, flag, flags, a_ss, a_rs, c_ss, c_rs, ch_ss, ch_rs, f_ss, f_rs, up_ss, up_rs, down_ss, down_rs, z_ss, z_rs, zm_ss, zm_rs,
           r_ss, r_rs, d_ss, d_rs, e_ss, e_rs, here, home):
    rep, gz = lax.axis_index("rep"), lax.axis_index("gz")
    y, z = rep // 4, gz // 2
    q = (gz % 2) * 4 + rep % 4
    slot, half = rep % 4, gz % 2

    inner = pl.ds(0, ROWS)
    first, last = pl.ds(0, PAD), pl.ds(ROWS - PAD, PAD)
    high, low = pl.ds(ROWS, PAD), pl.ds(ROWS + PAD, PAD)
    beside_inner = pl.ds(ROWS, 2 * PAD)

    def place(ring, row, depth):
        return (row * 4 + ring % 4, depth * 2 + ring // 4)

    def ring(step):
        return place((q + step + 8) % 8, y, z)

    above, below = place(q, (y + 1) % 4, z), place(q, (y + 3) % 4, z)
    z_next, z_last = place(q, y, (z + 1) % 8), place(q, y, (z + 7) % 8)

    def remote(src, dst, ss, rs, device):
        return pltpu.make_async_remote_copy(src_ref=src, dst_ref=dst, send_sem=ss, recv_sem=rs, device_id=device, device_id_type=MESH)

    loads = [[], []]
    for n, (src, dst) in enumerate(((field, fields), (momenta, slab))):
        for side in range(2):
            loads[n].append(pltpu.make_async_copy(src.at[0, :, :, pl.ds(side * LANES, LANES)], dst.at[:, side], here.at[n, side]))
            loads[n][side].start()

    barrier = pltpu.get_barrier_semaphore()
    partners = [ring(step) for step in range(1, 8)] + [above, below, z_next, z_last]
    for device in partners:
        pl.semaphore_signal(barrier, inc=1, device_id=device, device_id_type=MESH)
    pl.semaphore_wait(barrier, len(partners))

    def rows_of(place_):
        return pl.ds(pl.multiple_of(place_ * ROWS, ROWS), ROWS)

    def local_plane(pair):
        return pair + half * (3 - 2 * pair)

    def field_copy(pair, step):
        src = fields.at[local_plane(pair), :, rows_of((q + step) % 8)]
        dst = own.at[pair, half, slot]
        if step == 0:
            return pltpu.make_async_copy(src, dst, a_rs.at[pair, 0])
        return remote(src, dst, a_ss.at[pair, step], a_rs.at[pair, step], ring(step))

    def momenta_copy(pair, step):
        src = slab.at[local_plane(pair), :, rows_of((q + step) % 8)]
        dst = mom.at[slot, 4 + half * 4 + local_plane(pair), :, inner]
        if step == 0:
            return pltpu.make_async_copy(src, dst, c_rs.at[pair, 0])
        return remote(src, dst, c_ss.at[pair, step], c_rs.at[pair, step], ring(step))

    def edge_copy(step):
        src, dst = edges.at[step], mom.at[slot, pl.ds(4 + half * 4, 4), :, beside_inner]
        if step == 0:
            return pltpu.make_async_copy(src, dst, ch_rs.at[0])
        return remote(src, dst, ch_ss.at[step], ch_rs.at[step], ring(step))

    def fill_edges():
        upper = lax.broadcasted_iota(jnp.int32, (2, 8, LANES), 1) < PAD
        for step in range(8):
            base = ((q + step) % 8) * ROWS
            after = pl.ds(pl.multiple_of((base + ROWS) % SIDE, 8), 8)
            ahead = pl.ds(pl.multiple_of((base + SIDE - 8) % SIDE, 8), 8)
            for plane in range(4):
                edges[step, plane] = jnp.where(upper, slab[plane, :, after, :], slab[plane, :, ahead, :])

    def flag_copy(step):
        if step == 0:
            return pltpu.make_async_copy(flag, flags.at[q], f_rs.at[0])
        return remote(flag, flags.at[q], f_ss.at[step], f_rs.at[step], ring(step))

    for load in loads[0]:
        load.wait()
    for step in range(8):
        field_copy(0, step).start()
    flag[...] = jnp.full(flag.shape, accept[0], jnp.int32)
    for step in range(8):
        flag_copy(step).start()

    alive = [[(counts[4 * ((y + d) % 4) + i] > 0).astype(jnp.int32) for i in range(4)] for d in range(4)]
    before = [[sum(alive[d][:i], jnp.int32(0)) for i in range(4)] for d in range(4)]
    total = [sum(alive[d], jnp.int32(0)) for d in range(4)]
    mine = [jnp.int32(-1)] * 4
    for c in range(4):
        for i in range(4):
            mine[c] = jnp.where((alive[0][i] == 1) & (before[0][i] == c), i, mine[c])
    split_up = jnp.minimum(total[3], 4 - total[2])
    split = jnp.minimum(total[2], 4 - total[1])
    cum, parent = jnp.int32(0), [jnp.int32(0)] * SLOTS
    for r in range(16):
        cum = cum + counts[r]
        for s in range(SLOTS):
            parent[s] = parent[s] + (cum <= 4 * y + s).astype(jnp.int32)
    code = []
    for s in range(SLOTS):
        value = jnp.int32(0)
        for d in range(4):
            for i in range(4):
                k = before[d][i]
                if d == 0:
                    way = jnp.int32(i)
                elif d == 1:
                    way = 4 + k
                elif d == 3:
                    way = 8 + k
                else:
                    way = jnp.where(k < split, 12 + total[1] + k, 16 + total[3] + k - split)
                value = jnp.where(parent[s] == 4 * ((y + d) % 4) + i, way, value)
        code.append(value)

    def same(value, number):
        return jnp.full((2, 8, LANES), value, jnp.int32) == number

    def octet(t):
        turn = t % 4
        return t // 4, pl.ds(pl.multiple_of(jnp.where(turn == 0, 0, jnp.where(turn == 1, 24, turn * 8 - 8)), 8), 8)

    def assemble(t, forward):
        pair, rows = octet(jnp.minimum(t, CHUNKS - 1))
        for c in range(4):
            own_here = [same(mine[c], i) for i in range(4)]
            down_here = [same(total[0], c - f) for f in range(c + 1)]
            up_here = [same(split_up + c - total[0], f) for f in range(4)]
            for h in range(2):
                pieces = [own[pair, h, i, :, rows, :] for i in range(4)]
                if forward:
                    down, up = from_above[t - LAG, 0, h], from_below[t - LAG, 0, h]
                    for f in range(1, c + 1):
                        down = jnp.where(down_here[f], from_above[t - LAG, f, h], down)
                    for f in range(1, 4):
                        up = jnp.where(up_here[f], from_below[t - LAG, f, h], up)
                else:
                    down = up = pieces[0]
                for i in range(4):
                    down = jnp.where(own_here[i], pieces[i], down)
                    up = jnp.where(own_here[i], pieces[i], up)
                send_down[t, c, h] = down
                send_up[t, c, h] = up

    def up_copy(t):
        return remote(send_up.at[t], from_below.at[t], up_ss.at[t], up_rs.at[t], above)

    def down_copy(t):
        return remote(send_down.at[t], from_above.at[t], down_ss.at[t], down_rs.at[t], below)

    def pick(u):
        pair, rows = octet(u)
        for s in range(SLOTS):
            here_ = [same(code[s], k) for k in range(20)]
            for h in range(2):
                value = own[pair, h, 0, :, rows, :]
                for i in range(1, 4):
                    value = jnp.where(here_[i], own[pair, h, i, :, rows, :], value)
                for c in range(4):
                    value = jnp.where(here_[4 + c], from_above[u, c, h], value)
                    value = jnp.where(here_[8 + c], from_below[u, c, h], value)
                    value = jnp.where(here_[12 + c], from_above[u + LAG, c, h], value)
                    value = jnp.where(here_[16 + c], from_below[u + LAG, c, h], value)
                plane = 4 + pair if h == 0 else 11 - pair
                phi0[s, plane, :, rows, :] = value

    def z_copies(pair):
        return (
            remote(phi0.at[:, 4 + pair], phi0.at[:, 12 + pair], z_ss.at[pair, 0], z_rs.at[pair, 0], z_last),
            remote(phi0.at[:, 11 - pair], phi0.at[:, 3 - pair], z_ss.at[pair, 1], z_rs.at[pair, 1], z_next),
        )

    zm_copies = (
        remote(mom.at[:, 4], mom.at[:, 12], zm_ss.at[0], zm_rs.at[0], z_last),
        remote(mom.at[:, 11], mom.at[:, 3], zm_ss.at[1], zm_rs.at[1], z_next),
    )

    def row_copies(pair):
        copies = []
        for n, plane in enumerate((4 + pair, 11 - pair)):
            copies.append(remote(phi0.at[:, plane, :, first], phi0.at[:, plane, :, high], r_ss.at[pair, n, 0], r_rs.at[pair, n, 0], ring(-1)))
            copies.append(remote(phi0.at[:, plane, :, last], phi0.at[:, plane, :, low], r_ss.at[pair, n, 1], r_rs.at[pair, n, 1], ring(1)))
        return copies

    def tick(t, carry):
        @pl.when(t < 3)
        def _():
            for step in range(8):
                field_copy(t + 1, step).start()

        @pl.when((t % 4 == 0) & (t < CHUNKS))
        def _():
            for step in range(8):
                copy = field_copy(t // 4, step)
                copy.wait() if step == 0 else copy.wait_recv()

        @pl.when(t >= LAG)
        def _():
            up_copy(t - LAG).wait_recv()
            down_copy(t - LAG).wait_recv()

        @pl.when(t < LAG)
        def _():
            assemble(t, False)

        @pl.when((t >= LAG) & (t < MESSAGES))
        def _():
            assemble(t, True)

        @pl.when(t < MESSAGES)
        def _():
            up_copy(t).start()
            down_copy(t).start()

        @pl.when(t == 4)
        def _():
            for load in loads[1]:
                load.wait()
            fill_edges()
            for step in range(8):
                edge_copy(step).start()

        @pl.when((t >= 6) & (t < 14) & (t % 2 == 0))
        def _():
            for step in range(8):
                momenta_copy((t - 6) // 2, step).start()

        @pl.when(t >= 2 * LAG)
        def _():
            pick(t - 2 * LAG)

        @pl.when((t >= 2 * LAG + 1) & ((t - 2 * LAG) % 4 == 1))
        def _():
            for copy in row_copies((t - 2 * LAG - 1) // 4):
                copy.start()

        @pl.when((t == 2 * LAG + 3) | (t == 2 * LAG + 7))
        def _():
            pair = (t - 2 * LAG - 3) // 4
            for copy in row_copies(pair):
                copy.wait_recv()
            for copy in z_copies(pair):
                copy.start()

        @pl.when(t == 12)
        def _():
            for step in range(8):
                for copy in (edge_copy(step), momenta_copy(0, step)):
                    copy.wait() if step == 0 else copy.wait_recv()
            for copy in zm_copies:
                copy.start()

        return carry

    lax.fori_loop(0, MESSAGES + LAG, tick, 0)

    for pair in range(1, PAIRS):
        for step in range(8):
            copy = momenta_copy(pair, step)
            copy.wait() if step == 0 else copy.wait_recv()
    for step in range(8):
        copy = flag_copy(step)
        copy.wait() if step == 0 else copy.wait_recv()
    for copy in zm_copies:
        copy.wait()
    for pair in range(2):
        for copy in z_copies(pair):
            copy.wait_recv()
    for copy in row_copies(2) + row_copies(3):
        copy.wait_recv()

    def end_copies(k, s):
        src, n = (phi2, phi3)[k - 2].at[s], k - 2
        return (
            remote(src.at[0], sides.at[n, s, 1], d_ss.at[n, s, 0], d_rs.at[n, s, 0], z_last),
            remote(src.at[7], sides.at[n, s, 0], d_ss.at[n, s, 1], d_rs.at[n, s, 1], z_next),
        )

    PARTS = ((2, 2), (1, 1), (0, 1))

    def result_copy(s, h, part, away):
        first_plane, number = PARTS[part]
        src = done.at[s, pl.ds(8 - number - first_plane if h else first_plane, number)]
        dst = out.at[0, pl.ds(4 - number - first_plane if h else first_plane, number), rows_of(q)]
        if away:
            return remote(src, dst, e_ss.at[s, h, part], e_rs.at[part, q], place(4 * h + s, y, z))
        return pltpu.make_async_copy(src, dst, home.at[part])

    def results(s, part, act):
        for h in range(2):
            @pl.when(q == 4 * h + s)
            def _():
                act(result_copy(s, h, part, False), False)

            @pl.when(q != 4 * h + s)
            def _():
                act(result_copy(s, h, part, True), True)

    tiles = range(ALL // 8)

    def spread(t):
        return pl.ds(t, 8, stride=ALL // 8)

    edge_lane = lax.broadcasted_iota(jnp.int32, (8, LANES), 1)
    first_lane, last_lane = edge_lane == 0, edge_lane == LANES - 1

    def natural(ref, plane):
        return [[ref[plane, n, spread(t), :] for t in tiles] for n in range(2)]

    def packed(ref, plane):
        return [[ref[plane, n, 8 * t:8 * t + 8, :] for t in tiles] for n in range(2)]

    def keep(ref, plane, values):
        for n in range(2):
            for t in tiles:
                ref[plane, n, 8 * t:8 * t + 8, :] = values[n][t]

    def each(act, *args):
        return [[act(*(arg[n][t] for arg in args)) for t in tiles] for n in range(2)]

    def kick(below_, centre, above_, scale):
        back = [[pltpu.roll(centre[n][t], 1, 1) for t in tiles] for n in range(2)]
        fore = [[pltpu.roll(centre[n][t], LANES - 1, 1) for t in tiles] for n in range(2)]
        result = [[], []]
        for n in range(2):
            for t in tiles:
                c = centre[n][t]
                ahead = centre[n][t - 1] if t > 0 else pltpu.roll(centre[n][-1], 1, 0)
                after = centre[n][t + 1] if t < len(tiles) - 1 else pltpu.roll(centre[n][0], 7, 0)
                left_ = jnp.where(first_lane, back[1 - n][t], back[n][t])
                right_ = jnp.where(last_lane, fore[1 - n][t], fore[n][t])
                beside = (below_[n][t] + above_[n][t]) + (ahead + after) + (left_ + right_)
                result[n].append((scale * 2.0 * KAPPA) * beside + c * (scale * (4.0 * LAMBDA - 2.0) - (scale * 4.0 * LAMBDA) * (c * c)))
        return result

    def finish(s, taken, plane, trio, move):
        push = kick(*trio, EPS * EPS)
        start = natural(phi0.at[s], 4 + plane)
        value = each(lambda c, m, f, b: jnp.where(taken, c + (m + f), b), trio[1], move, push, start)
        for n in range(2):
            for t in tiles:
                turned[plane, n, spread(t), :] = value[n][t]
            done[s, plane, :, n * LANES:(n + 1) * LANES] = turned[plane, n, :ROWS, :]

    def advance(trio, move, scale=EPS * EPS):
        push = kick(*trio, scale)
        move = each(lambda m, f: m + f, move, push)
        return move, each(lambda c, m: c + m, trio[1], move)

    def one_slot(n, carry):
        s = (n % 2) * 2 + n // 2
        taken = flags[s] == 1
        start, second, third, held = phi0.at[s], phi2.at[s], phi3.at[s], moves.at[s]
        trio = [None, natural(start, 2), natural(start, 3)]
        for plane in range(3, 13):
            trio = trio[1:] + [natural(start, plane + 1)]
            move = each(lambda m: EPS * m, natural(mom.at[s], plane))
            move, value = advance(trio, move, 0.5 * EPS * EPS)
            if 4 <= plane < 12:
                keep(held, plane - 4, move)
            keep(phi1, plane - 3, value)
        trio = [None, packed(phi1, 0), packed(phi1, 1)]
        for plane in range(8):
            trio = trio[1:] + [packed(phi1, plane + 2)]
            move, value = advance(trio, packed(held, plane))
            keep(held, plane, move)
            keep(second, plane, value)
        for copy in end_copies(2, s):
            copy.start()
        trio = [None, packed(second, 0), packed(second, 1)]
        for plane in range(1, 7):
            trio = trio[1:] + [packed(second, plane + 1)]
            move, value = advance(trio, packed(held, plane))
            keep(held, plane, move)
            keep(third, plane, value)
        trio = [None, packed(third, 1), packed(third, 2)]
        for plane in range(2, 6):
            trio = trio[1:] + [packed(third, plane + 1)]
            finish(s, taken, plane, trio, packed(held, plane))
        results(s, 0, lambda copy, away: copy.start())
        return carry

    def next_planes(n, carry):
        s = (n % 2) * 2 + n // 2
        taken = flags[s] == 1
        second, third, held, beyond = phi2.at[s], phi3.at[s], moves.at[s], sides.at[0, s]
        for copy in end_copies(2, s):
            copy.wait_recv()
        for plane in (0, 7):
            inside = packed(second, 1 if plane == 0 else 6)
            move, value = advance([packed(beyond, plane // 7), packed(second, plane), inside], packed(held, plane))
            keep(held, plane, move)
            keep(third, plane, value)
        for copy in end_copies(3, s):
            copy.start()
        for plane in (1, 6):
            finish(s, taken, plane, [packed(third, plane + n_) for n_ in (-1, 0, 1)], packed(held, plane))
        results(s, 1, lambda copy, away: copy.start())
        return carry

    def end_planes(n, carry):
        s = (n % 2) * 2 + n // 2
        taken = flags[s] == 1
        third, held, beyond = phi3.at[s], moves.at[s], sides.at[1, s]
        for copy in end_copies(3, s):
            copy.wait_recv()
        for plane in (0, 7):
            inside = packed(third, 1 if plane == 0 else 6)
            finish(s, taken, plane, [packed(beyond, plane // 7), packed(third, plane), inside], packed(held, plane))
        results(s, 2, lambda copy, away: copy.start())
        return carry

    lax.fori_loop(0, SLOTS, one_slot, 0)
    lax.fori_loop(0, SLOTS, next_planes, 0)
    lax.fori_loop(0, SLOTS, end_planes, 0)

    for pair in range(PAIRS):
        for step in range(1, 8):
            field_copy(pair, step).wait_send()
            momenta_copy(pair, step).wait_send()
        for copy in row_copies(pair):
            copy.wait_send()
    for pair in range(2):
        for copy in z_copies(pair):
            copy.wait_send()
    for step in range(1, 8):
        flag_copy(step).wait_send()
        edge_copy(step).wait_send()

    def left(t, carry):
        up_copy(t).wait_send()
        down_copy(t).wait_send()
        return carry

    lax.fori_loop(0, MESSAGES, left, 0)
    for s in range(SLOTS):
        for copy in end_copies(2, s) + end_copies(3, s):
            copy.wait_send()
        for part in range(3):
            results(s, part, lambda copy, away: copy.wait_send() if away else copy.wait())
    for part in range(3):
        for step in range(1, 8):
            origin = (q + 8 - step) % 8
            size = pl.ds(0, PARTS[part][1])
            remote(done.at[0, size], out.at[0, size, rows_of(origin)], e_ss.at[0, 0, 0], e_rs.at[part, origin], ring(step)).wait_recv()


def local(field, momenta, counts, accept):
    f32, dma = jnp.float32, pltpu.SemaphoreType.DMA
    message = (MESSAGES, 4, 2, 2, 8, LANES)
    plane = (2, ALL, LANES)
    return pl.pallas_call(
        kernel,
        out_shape=jax.ShapeDtypeStruct(field.shape, f32),
        in_specs=[
            pl.BlockSpec(memory_space=pltpu.HBM),
            pl.BlockSpec(memory_space=pltpu.HBM),
            pl.BlockSpec(memory_space=pltpu.SMEM),
            pl.BlockSpec(memory_space=pltpu.SMEM),
        ],
        out_specs=pl.BlockSpec(memory_space=pltpu.VMEM),
        scratch_shapes=[
            pltpu.VMEM((PAIRS, 2, SLOTS, 2, ROWS, LANES), f32),
            pltpu.VMEM(message, f32),
            pltpu.VMEM(message, f32),
            pltpu.VMEM(message, f32),
            pltpu.VMEM(message, f32),
            pltpu.VMEM((SLOTS, 16) + plane, f32),
            pltpu.VMEM((10,) + plane, f32),
            pltpu.VMEM((SLOTS, 8) + plane, f32),
            pltpu.VMEM((SLOTS, 8) + plane, f32),
            pltpu.VMEM((SLOTS, 16) + plane, f32),
            pltpu.VMEM((SLOTS, 8) + plane, f32),
            pltpu.VMEM((2, SLOTS, 2) + plane, f32),
            pltpu.VMEM((SLOTS, 8, ROWS, SIDE), f32),
            pltpu.VMEM((8,) + plane, f32),
            pltpu.VMEM((4, 2, SIDE, LANES), f32),
            pltpu.VMEM((4, 2, SIDE, LANES), f32),
            pltpu.VMEM((8, 4, 2, 8, LANES), f32),
            pltpu.VMEM((8, LANES), jnp.int32),
            pltpu.VMEM((8, 8, LANES), jnp.int32),
            dma((PAIRS, 8)), dma((PAIRS, 8)), dma((PAIRS, 8)), dma((PAIRS, 8)), dma((8,)), dma((8,)), dma((8,)), dma((8,)),
            dma((MESSAGES,)), dma((MESSAGES,)), dma((MESSAGES,)), dma((MESSAGES,)),
            dma((2, 2)), dma((2, 2)), dma((2,)), dma((2,)),
            dma((PAIRS, 2, 2)), dma((PAIRS, 2, 2)), dma((2, SLOTS, 2)), dma((2, SLOTS, 2)), dma((SLOTS, 2, 3)), dma((3, 8)), dma((2, 2)), dma((3,)),
        ],
        compiler_params=pltpu.CompilerParams(collective_id=0, has_side_effects=True, vmem_limit_bytes=52 * 1024 * 1024),
    )(field, momenta, counts, accept)


def solution(mesh):
    placed = (P("rep", "gz", None, None), P("rep", "gz", None, None), P(), P("rep"))
    return jax.shard_map(
        local, mesh=mesh, in_specs=placed, out_specs=P("rep", "gz", None, None), check_vma=False
    )
```

```python
import jax
import jax.numpy as jnp
from jax import lax
from jax.experimental import pallas as pl
from jax.experimental.pallas import tpu as pltpu
from jax.sharding import PartitionSpec as P

KAPPA = 0.16
LAMBDA = 0.015
EPS = 0.75

MESH = pl.DeviceIdType.MESH
SLOTS = 4
ROWS = 32
PAD = 4
ALL = ROWS + 2 * PAD
SIDE = 256
LANES = 128
PAIRS = 4
CHUNKS = 16
LAG = 3
MESSAGES = CHUNKS + LAG


def kernel(field, momenta, counts, accept, out, own, send_up, send_down, from_below, from_above, phi0, phi1, phi2, phi3, mom, moves, sides,
           done, turned, fields, slab, edges, flag, flags, a_ss, a_rs, c_ss, c_rs, ch_ss, ch_rs, f_ss, f_rs, up_ss, up_rs, down_ss, down_rs, z_ss, z_rs, zm_ss, zm_rs,
           r_ss, r_rs, d_ss, d_rs, e_ss, e_rs, here):
    rep, gz = lax.axis_index("rep"), lax.axis_index("gz")
    y, z = rep // 4, gz // 2
    q = (gz % 2) * 4 + rep % 4
    slot, half = rep % 4, gz % 2

    inner = pl.ds(0, ROWS)
    first, last = pl.ds(0, PAD), pl.ds(ROWS - PAD, PAD)
    high, low = pl.ds(ROWS, PAD), pl.ds(ROWS + PAD, PAD)
    beside_inner = pl.ds(ROWS, 2 * PAD)

    def place(ring, row, depth):
        return (row * 4 + ring % 4, depth * 2 + ring // 4)

    def ring(step):
        return place((q + step + 8) % 8, y, z)

    above, below = place(q, (y + 1) % 4, z), place(q, (y + 3) % 4, z)
    z_next, z_last = place(q, y, (z + 1) % 8), place(q, y, (z + 7) % 8)

    def remote(src, dst, ss, rs, device):
        return pltpu.make_async_remote_copy(src_ref=src, dst_ref=dst, send_sem=ss, recv_sem=rs, device_id=device, device_id_type=MESH)

    def took(like, sem):
        pltpu.make_async_copy(like, like, sem).wait()

    for n, (src, dst) in enumerate(((field, fields), (momenta, slab))):
        for side in range(2):
            pltpu.make_async_copy(src.at[0, :, :, pl.ds(side * LANES, LANES)], dst.at[:, side], here.at[n]).start()

    barrier = pltpu.get_barrier_semaphore()
    partners = [ring(step) for step in range(1, 8)] + [above, below, z_next, z_last]
    for device in partners:
        pl.semaphore_signal(barrier, inc=1, device_id=device, device_id_type=MESH)
    pl.semaphore_wait(barrier, len(partners))

    def rows_of(place_):
        return pl.ds(pl.multiple_of(place_ * ROWS, ROWS), ROWS)

    def local_plane(pair):
        return pair + half * (3 - 2 * pair)

    def field_copy(pair, step):
        src = fields.at[local_plane(pair), :, rows_of((q + step) % 8)]
        dst = own.at[pair, half, slot]
        if step == 0:
            return pltpu.make_async_copy(src, dst, a_rs.at[pair])
        return remote(src, dst, a_ss, a_rs.at[pair], ring(step))

    def momenta_copy(pair, step):
        src = slab.at[local_plane(pair), :, rows_of((q + step) % 8)]
        dst = mom.at[slot, 4 + half * 4 + local_plane(pair), :, inner]
        if step == 0:
            return pltpu.make_async_copy(src, dst, c_rs.at[pair])
        return remote(src, dst, c_ss, c_rs.at[pair], ring(step))

    def edge_copy(step):
        src, dst = edges.at[step], mom.at[slot, pl.ds(4 + half * 4, 4), :, beside_inner]
        if step == 0:
            return pltpu.make_async_copy(src, dst, ch_rs)
        return remote(src, dst, ch_ss, ch_rs, ring(step))

    def fill_edges():
        upper = lax.broadcasted_iota(jnp.int32, (2, 8, LANES), 1) < PAD
        for step in range(8):
            base = ((q + step) % 8) * ROWS
            after = pl.ds(pl.multiple_of((base + ROWS) % SIDE, 8), 8)
            ahead = pl.ds(pl.multiple_of((base + SIDE - 8) % SIDE, 8), 8)
            for plane in range(4):
                edges[step, plane] = jnp.where(upper, slab[plane, :, after, :], slab[plane, :, ahead, :])

    def flag_copy(step):
        if step == 0:
            return pltpu.make_async_copy(flag, flags.at[q], f_rs)
        return remote(flag, flags.at[q], f_ss, f_rs, ring(step))

    took(fields, here.at[0])
    for step in range(8):
        field_copy(0, step).start()
    flag[...] = jnp.full(flag.shape, accept[0], jnp.int32)

    alive = [[(counts[4 * ((y + d) % 4) + i] > 0).astype(jnp.int32) for i in range(4)] for d in range(4)]
    before = [[sum(alive[d][:i], jnp.int32(0)) for i in range(4)] for d in range(4)]
    total = [sum(alive[d], jnp.int32(0)) for d in range(4)]
    mine = [jnp.int32(-1)] * 4
    for c in range(4):
        for i in range(4):
            mine[c] = jnp.where((alive[0][i] == 1) & (before[0][i] == c), i, mine[c])
    split_up = jnp.minimum(total[3], 4 - total[2])
    split = jnp.minimum(total[2], 4 - total[1])
    cum, parent = jnp.int32(0), [jnp.int32(0)] * SLOTS
    for r in range(16):
        cum = cum + counts[r]
        for s in range(SLOTS):
            parent[s] = parent[s] + (cum <= 4 * y + s).astype(jnp.int32)
    code = []
    for s in range(SLOTS):
        value = jnp.int32(0)
        for d in range(4):
            for i in range(4):
                k = before[d][i]
                if d == 0:
                    way = jnp.int32(i)
                elif d == 1:
                    way = 4 + k
                elif d == 3:
                    way = 8 + k
                else:
                    way = jnp.where(k < split, 12 + total[1] + k, 16 + total[3] + k - split)
                value = jnp.where(parent[s] == 4 * ((y + d) % 4) + i, way, value)
        code.append(value)

    def same(value, number):
        return jnp.full((2, 8, LANES), value, jnp.int32) == number

    def octet(t):
        turn = t % 4
        return t // 4, pl.ds(pl.multiple_of(jnp.where(turn == 0, 0, jnp.where(turn == 1, 24, turn * 8 - 8)), 8), 8)

    def assemble(t, forward):
        pair, rows = octet(jnp.minimum(t, CHUNKS - 1))
        for c in range(4):
            own_here = [same(mine[c], i) for i in range(4)]
            down_here = [same(total[0], c - f) for f in range(c + 1)]
            up_here = [same(split_up + c - total[0], f) for f in range(4)]
            for h in range(2):
                pieces = [own[pair, h, i, :, rows, :] for i in range(4)]
                if forward:
                    down, up = from_above[t - LAG, 0, h], from_below[t - LAG, 0, h]
                    for f in range(1, c + 1):
                        down = jnp.where(down_here[f], from_above[t - LAG, f, h], down)
                    for f in range(1, 4):
                        up = jnp.where(up_here[f], from_below[t - LAG, f, h], up)
                else:
                    down = up = pieces[0]
                for i in range(4):
                    down = jnp.where(own_here[i], pieces[i], down)
                    up = jnp.where(own_here[i], pieces[i], up)
                send_down[t, c, h] = down
                send_up[t, c, h] = up

    def up_copy(t):
        return remote(send_up.at[t], from_below.at[t], up_ss, up_rs.at[t], above)

    def down_copy(t):
        return remote(send_down.at[t], from_above.at[t], down_ss, down_rs.at[t], below)

    def pick(u):
        pair, rows = octet(u)
        for s in range(SLOTS):
            here_ = [same(code[s], k) for k in range(20)]
            for h in range(2):
                value = own[pair, h, 0, :, rows, :]
                for i in range(1, 4):
                    value = jnp.where(here_[i], own[pair, h, i, :, rows, :], value)
                for c in range(4):
                    value = jnp.where(here_[4 + c], from_above[u, c, h], value)
                    value = jnp.where(here_[8 + c], from_below[u, c, h], value)
                    value = jnp.where(here_[12 + c], from_above[u + LAG, c, h], value)
                    value = jnp.where(here_[16 + c], from_below[u + LAG, c, h], value)
                plane = 4 + pair if h == 0 else 11 - pair
                phi0[s, plane, :, rows, :] = value

    def z_copies(pair):
        return (
            remote(phi0.at[:, 4 + pair], phi0.at[:, 12 + pair], z_ss, z_rs.at[pair], z_last),
            remote(phi0.at[:, 11 - pair], phi0.at[:, 3 - pair], z_ss, z_rs.at[pair], z_next),
        )

    zm_copies = (
        remote(mom.at[:, 4], mom.at[:, 12], zm_ss, zm_rs, z_last),
        remote(mom.at[:, 11], mom.at[:, 3], zm_ss, zm_rs, z_next),
    )

    def row_copies(pair):
        copies = []
        for n, plane in enumerate((4 + pair, 11 - pair)):
            copies.append(remote(phi0.at[:, plane, :, first], phi0.at[:, plane, :, high], r_ss, r_rs.at[pair], ring(-1)))
            copies.append(remote(phi0.at[:, plane, :, last], phi0.at[:, plane, :, low], r_ss, r_rs.at[pair], ring(1)))
        return copies

    momenta_pair = mom.at[:, pl.ds(4, 2), :, inner]
    row_halo = phi0.at[:, pl.ds(4, 2), :, beside_inner]

    def tick(t, carry):
        @pl.when(t < 3)
        def _():
            for step in range(8):
                field_copy(t + 1, step).start()

        @pl.when((t % 4 == 0) & (t < CHUNKS))
        def _():
            took(own.at[t // 4], a_rs.at[t // 4])

        @pl.when(t >= LAG)
        def _():
            up_copy(t - LAG).wait_recv()
            down_copy(t - LAG).wait_recv()

        @pl.when(t < LAG)
        def _():
            assemble(t, False)

        @pl.when((t >= LAG) & (t < MESSAGES))
        def _():
            assemble(t, True)

        @pl.when(t < MESSAGES)
        def _():
            up_copy(t).start()
            down_copy(t).start()

        @pl.when(t == 4)
        def _():
            took(slab, here.at[1])
            fill_edges()
            for step in range(8):
                edge_copy(step).start()
                flag_copy(step).start()

        @pl.when((t >= 6) & (t < 14) & (t % 2 == 0))
        def _():
            for step in range(8):
                momenta_copy((t - 6) // 2, step).start()

        @pl.when(t >= 2 * LAG)
        def _():
            pick(t - 2 * LAG)

        @pl.when((t >= 2 * LAG + 1) & ((t - 2 * LAG) % 4 == 1))
        def _():
            for copy in row_copies((t - 2 * LAG - 1) // 4):
                copy.start()

        @pl.when((t == 2 * LAG + 3) | (t == 2 * LAG + 7))
        def _():
            pair = (t - 2 * LAG - 3) // 4
            took(row_halo, r_rs.at[pair])
            for copy in z_copies(pair):
                copy.start()

        @pl.when(t == 12)
        def _():
            took(mom.at[:, pl.ds(4, 8), :, beside_inner], ch_rs)
            took(momenta_pair, c_rs.at[0])
            for copy in zm_copies:
                copy.start()

        return carry

    lax.fori_loop(0, MESSAGES + LAG, tick, 0)

    for pair in range(1, PAIRS):
        took(momenta_pair, c_rs.at[pair])
    took(flags, f_rs)
    took(mom.at[:, pl.ds(0, 2)], zm_rs)
    took(mom.at[:, pl.ds(0, 2)], zm_ss)
    for pair in range(2):
        took(phi0.at[:, pl.ds(0, 2)], z_rs.at[pair])
    for pair in range(2, PAIRS):
        took(row_halo, r_rs.at[pair])

    def end_copies(k, s):
        src, n = (phi2, phi3)[k - 2].at[s], k - 2
        return (
            remote(src.at[0], sides.at[n, s, 1], d_ss, d_rs.at[n, s], z_last),
            remote(src.at[7], sides.at[n, s, 0], d_ss, d_rs.at[n, s], z_next),
        )

    PARTS = ((2, 2), (1, 1), (0, 1))

    def result_copy(s, h, part, away):
        first_plane, number = PARTS[part]
        src = done.at[s, pl.ds(8 - number - first_plane if h else first_plane, number)]
        dst = out.at[0, pl.ds(4 - number - first_plane if h else first_plane, number), rows_of(q)]
        if away:
            return remote(src, dst, e_ss, e_rs, place(4 * h + s, y, z))
        return pltpu.make_async_copy(src, dst, e_rs)

    def results(s, part):
        for h in range(2):
            @pl.when(q == 4 * h + s)
            def _():
                result_copy(s, h, part, False).start()

            @pl.when(q != 4 * h + s)
            def _():
                result_copy(s, h, part, True).start()

    tiles = range(ALL // 8)

    def spread(t):
        return pl.ds(t, 8, stride=ALL // 8)

    edge_lane = lax.broadcasted_iota(jnp.int32, (8, LANES), 1)
    first_lane, last_lane = edge_lane == 0, edge_lane == LANES - 1

    def natural(ref, plane):
        return [[ref[plane, n, spread(t), :] for t in tiles] for n in range(2)]

    def packed(ref, plane):
        return [[ref[plane, n, 8 * t:8 * t + 8, :] for t in tiles] for n in range(2)]

    def keep(ref, plane, values):
        for n in range(2):
            for t in tiles:
                ref[plane, n, 8 * t:8 * t + 8, :] = values[n][t]

    def each(act, *args):
        return [[act(*(arg[n][t] for arg in args)) for t in tiles] for n in range(2)]

    def kick(below_, centre, above_, scale):
        back = [[pltpu.roll(centre[n][t], 1, 1) for t in tiles] for n in range(2)]
        fore = [[pltpu.roll(centre[n][t], LANES - 1, 1) for t in tiles] for n in range(2)]
        result = [[], []]
        for n in range(2):
            for t in tiles:
                c = centre[n][t]
                ahead = centre[n][t - 1] if t > 0 else pltpu.roll(centre[n][-1], 1, 0)
                after = centre[n][t + 1] if t < len(tiles) - 1 else pltpu.roll(centre[n][0], 7, 0)
                left_ = jnp.where(first_lane, back[1 - n][t], back[n][t])
                right_ = jnp.where(last_lane, fore[1 - n][t], fore[n][t])
                beside = (below_[n][t] + above_[n][t]) + (ahead + after) + (left_ + right_)
                result[n].append((scale * 2.0 * KAPPA) * beside + c * (scale * (4.0 * LAMBDA - 2.0) - (scale * 4.0 * LAMBDA) * (c * c)))
        return result

    def finish(s, taken, plane, trio, move):
        push = kick(*trio, EPS * EPS)
        start = natural(phi0.at[s], 4 + plane)
        value = each(lambda c, m, f, b: jnp.where(taken, c + (m + f), b), trio[1], move, push, start)
        for n in range(2):
            for t in tiles:
                turned[plane, n, spread(t), :] = value[n][t]
            done[s, plane, :, n * LANES:(n + 1) * LANES] = turned[plane, n, :ROWS, :]

    def advance(trio, move, scale=EPS * EPS):
        push = kick(*trio, scale)
        move = each(lambda m, f: m + f, move, push)
        return move, each(lambda c, m: c + m, trio[1], move)

    def one_slot(n, carry):
        s = (n % 2) * 2 + n // 2
        taken = flags[s] == 1
        start, second, third, held = phi0.at[s], phi2.at[s], phi3.at[s], moves.at[s]
        trio = [None, natural(start, 2), natural(start, 3)]
        for plane in range(3, 13):
            trio = trio[1:] + [natural(start, plane + 1)]
            move = each(lambda m: EPS * m, natural(mom.at[s], plane))
            move, value = advance(trio, move, 0.5 * EPS * EPS)
            if 4 <= plane < 12:
                keep(held, plane - 4, move)
            keep(phi1, plane - 3, value)
        trio = [None, packed(phi1, 0), packed(phi1, 1)]
        for plane in range(8):
            trio = trio[1:] + [packed(phi1, plane + 2)]
            move, value = advance(trio, packed(held, plane))
            keep(held, plane, move)
            keep(second, plane, value)
        for copy in end_copies(2, s):
            copy.start()
        trio = [None, packed(second, 0), packed(second, 1)]
        for plane in range(1, 7):
            trio = trio[1:] + [packed(second, plane + 1)]
            move, value = advance(trio, packed(held, plane))
            keep(held, plane, move)
            keep(third, plane, value)
        trio = [None, packed(third, 1), packed(third, 2)]
        for plane in range(2, 6):
            trio = trio[1:] + [packed(third, plane + 1)]
            finish(s, taken, plane, trio, packed(held, plane))
        results(s, 0)
        return carry

    def next_planes(n, carry):
        s = (n % 2) * 2 + n // 2
        taken = flags[s] == 1
        second, third, held, beyond = phi2.at[s], phi3.at[s], moves.at[s], sides.at[0, s]
        took(sides.at[0, s], d_rs.at[0, s])
        for plane in (0, 7):
            inside = packed(second, 1 if plane == 0 else 6)
            move, value = advance([packed(beyond, plane // 7), packed(second, plane), inside], packed(held, plane))
            keep(held, plane, move)
            keep(third, plane, value)
        for copy in end_copies(3, s):
            copy.start()
        for plane in (1, 6):
            finish(s, taken, plane, [packed(third, plane + n_) for n_ in (-1, 0, 1)], packed(held, plane))
        results(s, 1)
        return carry

    def end_planes(n, carry):
        s = (n % 2) * 2 + n // 2
        taken = flags[s] == 1
        third, held, beyond = phi3.at[s], moves.at[s], sides.at[1, s]
        took(sides.at[1, s], d_rs.at[1, s])
        for plane in (0, 7):
            inside = packed(third, 1 if plane == 0 else 6)
            finish(s, taken, plane, [packed(beyond, plane // 7), packed(third, plane), inside], packed(held, plane))
        results(s, 2)
        return carry

    lax.fori_loop(0, SLOTS, one_slot, 0)
    lax.fori_loop(0, SLOTS, next_planes, 0)
    lax.fori_loop(0, SLOTS, end_planes, 0)

    seven = pl.ds(0, 7 * ROWS)
    took(fields.at[:, :, seven], a_ss)
    took(slab.at[:, :, seven], c_ss)
    took(edges.at[pl.ds(0, 7)], ch_ss)
    took(flags.at[pl.ds(0, 7)], f_ss)
    took(send_up, up_ss)
    took(send_down, down_ss)
    took(phi0.at[:, pl.ds(0, 4)], z_ss)
    took(phi0.at[:, pl.ds(4, 8), :, beside_inner], r_ss)
    took(sides, d_ss)
    took(out.at[0, :, seven], e_ss)
    took(out, e_rs)


def local(field, momenta, counts, accept):
    f32, dma = jnp.float32, pltpu.SemaphoreType.DMA
    message = (MESSAGES, 4, 2, 2, 8, LANES)
    plane = (2, ALL, LANES)
    return pl.pallas_call(
        kernel,
        out_shape=jax.ShapeDtypeStruct(field.shape, f32),
        in_specs=[
            pl.BlockSpec(memory_space=pltpu.HBM),
            pl.BlockSpec(memory_space=pltpu.HBM),
            pl.BlockSpec(memory_space=pltpu.SMEM),
            pl.BlockSpec(memory_space=pltpu.SMEM),
        ],
        out_specs=pl.BlockSpec(memory_space=pltpu.VMEM),
        scratch_shapes=[
            pltpu.VMEM((PAIRS, 2, SLOTS, 2, ROWS, LANES), f32),
            pltpu.VMEM(message, f32),
            pltpu.VMEM(message, f32),
            pltpu.VMEM(message, f32),
            pltpu.VMEM(message, f32),
            pltpu.VMEM((SLOTS, 16) + plane, f32),
            pltpu.VMEM((10,) + plane, f32),
            pltpu.VMEM((SLOTS, 8) + plane, f32),
            pltpu.VMEM((SLOTS, 8) + plane, f32),
            pltpu.VMEM((SLOTS, 16) + plane, f32),
            pltpu.VMEM((SLOTS, 8) + plane, f32),
            pltpu.VMEM((2, SLOTS, 2) + plane, f32),
            pltpu.VMEM((SLOTS, 8, ROWS, SIDE), f32),
            pltpu.VMEM((8,) + plane, f32),
            pltpu.VMEM((4, 2, SIDE, LANES), f32),
            pltpu.VMEM((4, 2, SIDE, LANES), f32),
            pltpu.VMEM((8, 4, 2, 8, LANES), f32),
            pltpu.VMEM((8, LANES), jnp.int32),
            pltpu.VMEM((8, 8, LANES), jnp.int32),
            dma, dma((PAIRS,)), dma, dma((PAIRS,)), dma, dma, dma, dma,
            dma, dma((MESSAGES,)), dma, dma((MESSAGES,)),
            dma, dma((2,)), dma, dma,
            dma, dma((PAIRS,)), dma, dma((2, SLOTS)), dma, dma, dma((2,)),
        ],
        compiler_params=pltpu.CompilerParams(collective_id=0, has_side_effects=True, vmem_limit_bytes=52 * 1024 * 1024),
    )(field, momenta, counts, accept)


def solution(mesh):
    placed = (P("rep", "gz", None, None), P("rep", "gz", None, None), P(), P("rep"))
    return jax.shard_map(
        local, mesh=mesh, in_specs=placed, out_specs=P("rep", "gz", None, None), check_vma=False
    )
```

```python
import jax
import jax.numpy as jnp
from jax import lax
from jax.experimental import pallas as pl
from jax.experimental.pallas import tpu as pltpu
from jax.sharding import PartitionSpec as P

KAPPA = 0.16
LAMBDA = 0.015
EPS = 0.75

MESH = pl.DeviceIdType.MESH
SLOTS = 4
ROWS = 32
PAD = 4
ALL = ROWS + 2 * PAD
SIDE = 256
LANES = 128
PAIRS = 4
CHUNKS = 16
LAG = 3
MESSAGES = CHUNKS + LAG


def kernel(field, momenta, counts_in, accept_in, out, own, send_up, send_down, from_below, from_above, phi0, phi1, phi2, phi3, mom, moves, sides,
           done, turned, fields, slab, edges, flag, flags, a_ss, a_rs, c_ss, c_rs, ch_ss, ch_rs, f_ss, f_rs, up_ss, down_ss, m_rs, z_ss, z_rs, zm_ss, zm_rs,
           r_ss, r_rs, d_ss, d_rs, e_ss, e_rs, here, counts, accept):
    rep, gz = lax.axis_index("rep"), lax.axis_index("gz")
    y, z = rep // 4, gz // 2
    q = (gz % 2) * 4 + rep % 4
    slot, half = rep % 4, gz % 2

    inner = pl.ds(0, ROWS)
    first, last = pl.ds(0, PAD), pl.ds(ROWS - PAD, PAD)
    high, low = pl.ds(ROWS, PAD), pl.ds(ROWS + PAD, PAD)
    beside_inner = pl.ds(ROWS, 2 * PAD)

    def place(ring, row, depth):
        return (row * 4 + ring % 4, depth * 2 + ring // 4)

    def ring(step):
        return place((q + step + 8) % 8, y, z)

    above, below = place(q, (y + 1) % 4, z), place(q, (y + 3) % 4, z)
    z_next, z_last = place(q, y, (z + 1) % 8), place(q, y, (z + 7) % 8)

    def remote(src, dst, ss, rs, device):
        return pltpu.make_async_remote_copy(src_ref=src, dst_ref=dst, send_sem=ss, recv_sem=rs, device_id=device, device_id_type=MESH)

    def took(like, sem):
        pltpu.make_async_copy(like, like, sem).wait()

    small = (pltpu.make_async_copy(counts_in, counts, here.at[2]), pltpu.make_async_copy(accept_in, accept, here.at[3]))
    for copy in small:
        copy.start()
    for n, (src, dst) in enumerate(((field, fields), (momenta, slab))):
        for side in range(2):
            pltpu.make_async_copy(src.at[0, :, :, pl.ds(side * LANES, LANES)], dst.at[:, side], here.at[n]).start()

    barrier = pltpu.get_barrier_semaphore()
    partners = [ring(step) for step in range(1, 8)] + [above, below, z_next, z_last]
    for device in partners:
        pl.semaphore_signal(barrier, inc=1, device_id=device, device_id_type=MESH)
    pl.semaphore_wait(barrier, len(partners))

    def rows_of(place_):
        return pl.ds(pl.multiple_of(place_ * ROWS, ROWS), ROWS)

    def local_plane(pair):
        return pair + half * (3 - 2 * pair)

    def field_copy(pair, step):
        src = fields.at[local_plane(pair), :, rows_of((q + step) % 8)]
        dst = own.at[pair, half, slot]
        if step == 0:
            return pltpu.make_async_copy(src, dst, a_rs.at[pair])
        return remote(src, dst, a_ss, a_rs.at[pair], ring(step))

    def first_copy(part, step):
        start = ((q + step) % 8) * ROWS + part * 16
        src = fields.at[local_plane(0), :, pl.ds(pl.multiple_of(start, 16), 16)]
        dst = own.at[0, half, slot, :, pl.ds(part * 16, 16)]
        if step == 0:
            return pltpu.make_async_copy(src, dst, a_rs.at[4 * part])
        return remote(src, dst, a_ss, a_rs.at[4 * part], ring(step))

    def momenta_copy(pair, step):
        src = slab.at[local_plane(pair), :, rows_of((q + step) % 8)]
        dst = mom.at[slot, 4 + half * 4 + local_plane(pair), :, inner]
        if step == 0:
            return pltpu.make_async_copy(src, dst, c_rs.at[pair])
        return remote(src, dst, c_ss, c_rs.at[pair], ring(step))

    def edge_copy(step):
        src, dst = edges.at[step], mom.at[slot, pl.ds(4 + half * 4, 4), :, beside_inner]
        if step == 0:
            return pltpu.make_async_copy(src, dst, ch_rs)
        return remote(src, dst, ch_ss, ch_rs, ring(step))

    def fill_edges():
        upper = lax.broadcasted_iota(jnp.int32, (2, 8, LANES), 1) < PAD
        for step in range(8):
            base = ((q + step) % 8) * ROWS
            after = pl.ds(pl.multiple_of((base + ROWS) % SIDE, 8), 8)
            ahead = pl.ds(pl.multiple_of((base + SIDE - 8) % SIDE, 8), 8)
            for plane in range(4):
                edges[step, plane] = jnp.where(upper, slab[plane, :, after, :], slab[plane, :, ahead, :])

    def flag_copy(step):
        if step == 0:
            return pltpu.make_async_copy(flag, flags.at[q], f_rs)
        return remote(flag, flags.at[q], f_ss, f_rs, ring(step))

    took(fields, here.at[0])
    for step in range(8):
        first_copy(0, step).start()
    for copy in small:
        copy.wait()
    flag[...] = jnp.full(flag.shape, accept[0], jnp.int32)

    alive = [[(counts[4 * ((y + d) % 4) + i] > 0).astype(jnp.int32) for i in range(4)] for d in range(4)]
    before = [[sum(alive[d][:i], jnp.int32(0)) for i in range(4)] for d in range(4)]
    total = [sum(alive[d], jnp.int32(0)) for d in range(4)]
    mine = [jnp.int32(-1)] * 4
    for c in range(4):
        for i in range(4):
            mine[c] = jnp.where((alive[0][i] == 1) & (before[0][i] == c), i, mine[c])
    split_up = jnp.minimum(total[3], 4 - total[2])
    split = jnp.minimum(total[2], 4 - total[1])
    cum, parent = jnp.int32(0), [jnp.int32(0)] * SLOTS
    for r in range(16):
        cum = cum + counts[r]
        for s in range(SLOTS):
            parent[s] = parent[s] + (cum <= 4 * y + s).astype(jnp.int32)
    code = []
    for s in range(SLOTS):
        value = jnp.int32(0)
        for d in range(4):
            for i in range(4):
                k = before[d][i]
                if d == 0:
                    way = jnp.int32(i)
                elif d == 1:
                    way = 4 + k
                elif d == 3:
                    way = 8 + k
                else:
                    way = jnp.where(k < split, 12 + total[1] + k, 16 + total[3] + k - split)
                value = jnp.where(parent[s] == 4 * ((y + d) % 4) + i, way, value)
        code.append(value)

    def same(value, number):
        return jnp.full((2, 8, LANES), value, jnp.int32) == number

    def octet(t):
        pair, turn = t // 4, t % 4
        outer = jnp.where(turn == 0, 0, jnp.where(turn == 1, 3, turn - 1))
        return pair, pl.ds(pl.multiple_of(jnp.where(pair == 0, turn, outer) * 8, 8), 8)

    def assemble(t, forward):
        pair, rows = octet(jnp.minimum(t, CHUNKS - 1))
        for c in range(4):
            own_here = [same(mine[c], i) for i in range(4)]
            down_here = [same(total[0], c - f) for f in range(c + 1)]
            up_here = [same(split_up + c - total[0], f) for f in range(4)]
            for h in range(2):
                pieces = [own[pair, h, i, :, rows, :] for i in range(4)]
                if forward:
                    down, up = from_above[t - LAG, 0, h], from_below[t - LAG, 0, h]
                    for f in range(1, c + 1):
                        down = jnp.where(down_here[f], from_above[t - LAG, f, h], down)
                    for f in range(1, 4):
                        up = jnp.where(up_here[f], from_below[t - LAG, f, h], up)
                else:
                    down = up = pieces[0]
                for i in range(4):
                    down = jnp.where(own_here[i], pieces[i], down)
                    up = jnp.where(own_here[i], pieces[i], up)
                send_down[t, c, h] = down
                send_up[t, c, h] = up

    def up_copy(t):
        return remote(send_up.at[t], from_below.at[t], up_ss, m_rs.at[t], above)

    def down_copy(t):
        return remote(send_down.at[t], from_above.at[t], down_ss, m_rs.at[t], below)

    def pick(u):
        pair, rows = octet(u)
        for s in range(SLOTS):
            here_ = [same(code[s], k) for k in range(20)]
            for h in range(2):
                value = own[pair, h, 0, :, rows, :]
                for i in range(1, 4):
                    value = jnp.where(here_[i], own[pair, h, i, :, rows, :], value)
                for c in range(4):
                    value = jnp.where(here_[4 + c], from_above[u, c, h], value)
                    value = jnp.where(here_[8 + c], from_below[u, c, h], value)
                    value = jnp.where(here_[12 + c], from_above[u + LAG, c, h], value)
                    value = jnp.where(here_[16 + c], from_below[u + LAG, c, h], value)
                plane = 4 + pair if h == 0 else 11 - pair
                phi0[s, plane, :, rows, :] = value

    def z_copies(pair):
        return (
            remote(phi0.at[:, 4 + pair], phi0.at[:, 12 + pair], z_ss, z_rs.at[pair], z_last),
            remote(phi0.at[:, 11 - pair], phi0.at[:, 3 - pair], z_ss, z_rs.at[pair], z_next),
        )

    zm_copies = (
        remote(mom.at[:, 4], mom.at[:, 12], zm_ss, zm_rs, z_last),
        remote(mom.at[:, 11], mom.at[:, 3], zm_ss, zm_rs, z_next),
    )

    def row_copies(pair):
        copies = []
        for n, plane in enumerate((4 + pair, 11 - pair)):
            copies.append(remote(phi0.at[:, plane, :, first], phi0.at[:, plane, :, high], r_ss, r_rs.at[pair], ring(-1)))
            copies.append(remote(phi0.at[:, plane, :, last], phi0.at[:, plane, :, low], r_ss, r_rs.at[pair], ring(1)))
        return copies

    momenta_pair = mom.at[:, pl.ds(4, 2), :, inner]
    row_halo = phi0.at[:, pl.ds(4, 2), :, beside_inner]

    def tick(t, carry):
        @pl.when(t == 0)
        def _():
            for step in range(8):
                first_copy(1, step).start()

        @pl.when((t < 5) & (t % 2 == 0))
        def _():
            for step in range(8):
                field_copy(t // 2 + 1, step).start()

        @pl.when((t == 0) | (t == 2))
        def _():
            took(own.at[0, :, :, :, pl.ds(0, 16)], a_rs.at[2 * t])

        @pl.when((t % 4 == 0) & (t > 0) & (t < CHUNKS))
        def _():
            took(own.at[t // 4], a_rs.at[t // 4])

        @pl.when(t >= LAG)
        def _():
            took(own.at[0, 0], m_rs.at[t - LAG])

        @pl.when(t < LAG)
        def _():
            assemble(t, False)

        @pl.when((t >= LAG) & (t < MESSAGES))
        def _():
            assemble(t, True)

        @pl.when(t < MESSAGES)
        def _():
            up_copy(t).start()
            down_copy(t).start()

        @pl.when(t == 6)
        def _():
            took(slab, here.at[1])
            fill_edges()
            for step in range(8):
                edge_copy(step).start()
                flag_copy(step).start()

        @pl.when((t >= 8) & (t < 16) & (t % 2 == 0))
        def _():
            for step in range(8):
                momenta_copy((t - 8) // 2, step).start()

        @pl.when(t >= 2 * LAG)
        def _():
            pick(t - 2 * LAG)

        @pl.when((t == 2 * LAG + 3) | (t == 2 * LAG + 5) | (t == 2 * LAG + 9) | (t == 2 * LAG + 13))
        def _():
            for copy in row_copies((t - 2 * LAG - 1) // 4):
                copy.start()

        @pl.when((t == 2 * LAG + 5) | (t == 2 * LAG + 7))
        def _():
            pair = (t - 2 * LAG - 5) // 2
            took(row_halo, r_rs.at[pair])
            for copy in z_copies(pair):
                copy.start()

        @pl.when(t == 14)
        def _():
            took(mom.at[:, pl.ds(4, 8), :, beside_inner], ch_rs)
            took(momenta_pair, c_rs.at[0])
            for copy in zm_copies:
                copy.start()

        return carry

    lax.fori_loop(0, MESSAGES + LAG, tick, 0)

    for pair in range(1, PAIRS):
        took(momenta_pair, c_rs.at[pair])
    took(flags, f_rs)
    took(mom.at[:, pl.ds(0, 2)], zm_rs)
    took(mom.at[:, pl.ds(0, 2)], zm_ss)
    for pair in range(2):
        took(phi0.at[:, pl.ds(0, 2)], z_rs.at[pair])
    for pair in range(2, PAIRS):
        took(row_halo, r_rs.at[pair])

    def end_copies(k, s):
        src, n = (phi2, phi3)[k - 2].at[s], k - 2
        return (
            remote(src.at[0], sides.at[n, s, 1], d_ss, d_rs.at[n, s], z_last),
            remote(src.at[7], sides.at[n, s, 0], d_ss, d_rs.at[n, s], z_next),
        )

    PARTS = ((2, 2), (1, 1), (0, 1))

    def result_copy(s, h, part, away):
        first_plane, number = PARTS[part]
        src = done.at[s, pl.ds(8 - number - first_plane if h else first_plane, number)]
        dst = out.at[0, pl.ds(4 - number - first_plane if h else first_plane, number), rows_of(q)]
        if away:
            return remote(src, dst, e_ss, e_rs, place(4 * h + s, y, z))
        return pltpu.make_async_copy(src, dst, e_rs)

    def results(s, part):
        for h in range(2):
            @pl.when(q == 4 * h + s)
            def _():
                result_copy(s, h, part, False).start()

            @pl.when(q != 4 * h + s)
            def _():
                result_copy(s, h, part, True).start()

    tiles = range(ALL // 8)

    def spread(t):
        return pl.ds(t, 8, stride=ALL // 8)

    edge_lane = lax.broadcasted_iota(jnp.int32, (8, LANES), 1)
    first_lane, last_lane = edge_lane == 0, edge_lane == LANES - 1

    def natural(ref, plane):
        return [[ref[plane, n, spread(t), :] for t in tiles] for n in range(2)]

    def packed(ref, plane):
        return [[ref[plane, n, 8 * t:8 * t + 8, :] for t in tiles] for n in range(2)]

    def keep(ref, plane, values):
        for n in range(2):
            for t in tiles:
                ref[plane, n, 8 * t:8 * t + 8, :] = values[n][t]

    def each(act, *args):
        return [[act(*(arg[n][t] for arg in args)) for t in tiles] for n in range(2)]

    def kick(below_, centre, above_, scale):
        back = [[pltpu.roll(centre[n][t], 1, 1) for t in tiles] for n in range(2)]
        fore = [[pltpu.roll(centre[n][t], LANES - 1, 1) for t in tiles] for n in range(2)]
        result = [[], []]
        for n in range(2):
            for t in tiles:
                c = centre[n][t]
                ahead = centre[n][t - 1] if t > 0 else pltpu.roll(centre[n][-1], 1, 0)
                after = centre[n][t + 1] if t < len(tiles) - 1 else pltpu.roll(centre[n][0], 7, 0)
                left_ = jnp.where(first_lane, back[1 - n][t], back[n][t])
                right_ = jnp.where(last_lane, fore[1 - n][t], fore[n][t])
                beside = (below_[n][t] + above_[n][t]) + (ahead + after) + (left_ + right_)
                result[n].append((scale * 2.0 * KAPPA) * beside + c * (scale * (4.0 * LAMBDA - 2.0) - (scale * 4.0 * LAMBDA) * (c * c)))
        return result

    def finish(s, taken, plane, trio, move):
        push = kick(*trio, EPS * EPS)
        start = natural(phi0.at[s], 4 + plane)
        value = each(lambda c, m, f, b: jnp.where(taken, c + (m + f), b), trio[1], move, push, start)
        for n in range(2):
            for t in tiles:
                turned[plane, n, spread(t), :] = value[n][t]
            done[s, plane, :, n * LANES:(n + 1) * LANES] = turned[plane, n, :ROWS, :]

    def advance(trio, move, scale=EPS * EPS):
        push = kick(*trio, scale)
        move = each(lambda m, f: m + f, move, push)
        return move, each(lambda c, m: c + m, trio[1], move)

    def one_slot(n, carry):
        s = (n % 2) * 2 + n // 2
        taken = flags[s] == 1
        start, second, third, held = phi0.at[s], phi2.at[s], phi3.at[s], moves.at[s]
        trio = [None, natural(start, 2), natural(start, 3)]
        for plane in range(3, 13):
            trio = trio[1:] + [natural(start, plane + 1)]
            move = each(lambda m: EPS * m, natural(mom.at[s], plane))
            move, value = advance(trio, move, 0.5 * EPS * EPS)
            if 4 <= plane < 12:
                keep(held, plane - 4, move)
            keep(phi1, plane - 3, value)
        trio = [None, packed(phi1, 0), packed(phi1, 1)]
        for plane in range(8):
            trio = trio[1:] + [packed(phi1, plane + 2)]
            move, value = advance(trio, packed(held, plane))
            keep(held, plane, move)
            keep(second, plane, value)
        for copy in end_copies(2, s):
            copy.start()
        trio = [None, packed(second, 0), packed(second, 1)]
        for plane in range(1, 7):
            trio = trio[1:] + [packed(second, plane + 1)]
            move, value = advance(trio, packed(held, plane))
            keep(held, plane, move)
            keep(third, plane, value)
        trio = [None, packed(third, 1), packed(third, 2)]
        for plane in range(2, 6):
            trio = trio[1:] + [packed(third, plane + 1)]
            finish(s, taken, plane, trio, packed(held, plane))
        results(s, 0)
        return carry

    def next_planes(n, carry):
        s = (n % 2) * 2 + n // 2
        taken = flags[s] == 1
        second, third, held, beyond = phi2.at[s], phi3.at[s], moves.at[s], sides.at[0, s]
        took(sides.at[0, s], d_rs.at[0, s])
        for plane in (0, 7):
            inside = packed(second, 1 if plane == 0 else 6)
            move, value = advance([packed(beyond, plane // 7), packed(second, plane), inside], packed(held, plane))
            keep(held, plane, move)
            keep(third, plane, value)
        for copy in end_copies(3, s):
            copy.start()
        for plane in (1, 6):
            finish(s, taken, plane, [packed(third, plane + n_) for n_ in (-1, 0, 1)], packed(held, plane))
        results(s, 1)
        return carry

    def end_planes(n, carry):
        s = (n % 2) * 2 + n // 2
        taken = flags[s] == 1
        third, held, beyond = phi3.at[s], moves.at[s], sides.at[1, s]
        took(sides.at[1, s], d_rs.at[1, s])
        for plane in (0, 7):
            inside = packed(third, 1 if plane == 0 else 6)
            finish(s, taken, plane, [packed(beyond, plane // 7), packed(third, plane), inside], packed(held, plane))
        results(s, 2)
        return carry

    lax.fori_loop(0, SLOTS, one_slot, 0)
    lax.fori_loop(0, SLOTS, next_planes, 0)
    lax.fori_loop(0, SLOTS, end_planes, 0)

    seven = pl.ds(0, 7 * ROWS)
    took(fields.at[:, :, seven], a_ss)
    took(slab.at[:, :, seven], c_ss)
    took(edges.at[pl.ds(0, 7)], ch_ss)
    took(flags.at[pl.ds(0, 7)], f_ss)
    took(send_up, up_ss)
    took(send_down, down_ss)
    took(phi0.at[:, pl.ds(0, 4)], z_ss)
    took(phi0.at[:, pl.ds(4, 8), :, beside_inner], r_ss)
    took(sides, d_ss)
    took(out.at[0, :, seven], e_ss)
    took(out, e_rs)


def local(field, momenta, counts, accept):
    f32, dma = jnp.float32, pltpu.SemaphoreType.DMA
    message = (MESSAGES, 4, 2, 2, 8, LANES)
    plane = (2, ALL, LANES)
    return pl.pallas_call(
        kernel,
        out_shape=jax.ShapeDtypeStruct(field.shape, f32),
        in_specs=[
            pl.BlockSpec(memory_space=pltpu.HBM),
            pl.BlockSpec(memory_space=pltpu.HBM),
            pl.BlockSpec(memory_space=pl.ANY),
            pl.BlockSpec(memory_space=pl.ANY),
        ],
        out_specs=pl.BlockSpec(memory_space=pltpu.VMEM),
        scratch_shapes=[
            pltpu.VMEM((PAIRS, 2, SLOTS, 2, ROWS, LANES), f32),
            pltpu.VMEM(message, f32),
            pltpu.VMEM(message, f32),
            pltpu.VMEM(message, f32),
            pltpu.VMEM(message, f32),
            pltpu.VMEM((SLOTS, 16) + plane, f32),
            pltpu.VMEM((10,) + plane, f32),
            pltpu.VMEM((SLOTS, 8) + plane, f32),
            pltpu.VMEM((SLOTS, 8) + plane, f32),
            pltpu.VMEM((SLOTS, 16) + plane, f32),
            pltpu.VMEM((SLOTS, 8) + plane, f32),
            pltpu.VMEM((2, SLOTS, 2) + plane, f32),
            pltpu.VMEM((SLOTS, 8, ROWS, SIDE), f32),
            pltpu.VMEM((8,) + plane, f32),
            pltpu.VMEM((4, 2, SIDE, LANES), f32),
            pltpu.VMEM((4, 2, SIDE, LANES), f32),
            pltpu.VMEM((8, 4, 2, 8, LANES), f32),
            pltpu.VMEM((8, LANES), jnp.int32),
            pltpu.VMEM((8, 8, LANES), jnp.int32),
            dma, dma((PAIRS + 1,)), dma, dma((PAIRS,)), dma, dma, dma, dma,
            dma, dma, dma((MESSAGES,)),
            dma, dma((2,)), dma, dma,
            dma, dma((PAIRS,)), dma, dma((2, SLOTS)), dma, dma, dma((4,)),
            pltpu.SMEM((16,), jnp.int32),
            pltpu.SMEM((1,), jnp.int32),
        ],
        compiler_params=pltpu.CompilerParams(collective_id=0, has_side_effects=True, vmem_limit_bytes=52 * 1024 * 1024),
    )(field, momenta, counts, accept)


def solution(mesh):
    placed = (P("rep", "gz", None, None), P("rep", "gz", None, None), P(), P("rep"))
    return jax.shard_map(
        local, mesh=mesh, in_specs=placed, out_specs=P("rep", "gz", None, None), check_vma=False
    )
```

```python
import jax
import jax.numpy as jnp
from jax import lax
from jax.experimental import pallas as pl
from jax.experimental.pallas import tpu as pltpu
from jax.sharding import PartitionSpec as P

KAPPA = 0.16
LAMBDA = 0.015
EPS = 0.75

MESH = pl.DeviceIdType.MESH
SLOTS = 4
ROWS = 32
PAD = 4
ALL = ROWS + 2 * PAD
SIDE = 256
LANES = 128
PAIRS = 4
CHUNKS = 16
LAG = 3
MESSAGES = CHUNKS + LAG


def kernel(field, momenta, counts_in, accept_in, out, own, send_up, send_down, from_below, from_above, phi0, phi1, phi2, phi3, mom, moves, sides,
           done, turned, fields, slab, edges, flag, flags, a_ss, a_rs, c_ss, c_rs, ch_ss, ch_rs, f_ss, f_rs, up_ss, down_ss, m_rs, z_ss, z_rs, zm_ss, zm_rs,
           r_ss, r_rs, d_ss, d_rs, e_ss, e_rs, here, counts, accept):
    rep, gz = lax.axis_index("rep"), lax.axis_index("gz")
    y, z = rep // 4, gz // 2
    q = (gz % 2) * 4 + rep % 4
    slot, half = rep % 4, gz % 2

    inner = pl.ds(0, ROWS)
    first, last = pl.ds(0, PAD), pl.ds(ROWS - PAD, PAD)
    high, low = pl.ds(ROWS, PAD), pl.ds(ROWS + PAD, PAD)
    beside_inner = pl.ds(ROWS, 2 * PAD)

    def place(ring, row, depth):
        return (row * 4 + ring % 4, depth * 2 + ring // 4)

    def ring(step):
        return place((q + step + 8) % 8, y, z)

    above, below = place(q, (y + 1) % 4, z), place(q, (y + 3) % 4, z)
    z_next, z_last = place(q, y, (z + 1) % 8), place(q, y, (z + 7) % 8)

    def remote(src, dst, ss, rs, device):
        return pltpu.make_async_remote_copy(src_ref=src, dst_ref=dst, send_sem=ss, recv_sem=rs, device_id=device, device_id_type=MESH)

    def took(like, sem):
        pltpu.make_async_copy(like, like, sem).wait()

    small = (pltpu.make_async_copy(counts_in, counts, here.at[2]), pltpu.make_async_copy(accept_in, accept, here.at[3]))
    for copy in small:
        copy.start()
    for n, (src, dst) in enumerate(((field, fields), (momenta, slab))):
        for side in range(2):
            pltpu.make_async_copy(src.at[0, :, :, pl.ds(side * LANES, LANES)], dst.at[:, side], here.at[n]).start()

    barrier = pltpu.get_barrier_semaphore()
    partners = [ring(step) for step in range(1, 8)] + [above, below, z_next, z_last]
    for device in partners:
        pl.semaphore_signal(barrier, inc=1, device_id=device, device_id_type=MESH)
    pl.semaphore_wait(barrier, len(partners))

    def rows_of(place_):
        return pl.ds(pl.multiple_of(place_ * ROWS, ROWS), ROWS)

    def local_plane(pair):
        return pair + half * (3 - 2 * pair)

    def field_copy(pair, step):
        src = fields.at[local_plane(pair), :, rows_of((q + step) % 8)]
        dst = own.at[pair, half, slot]
        if step == 0:
            return pltpu.make_async_copy(src, dst, a_rs.at[pair])
        return remote(src, dst, a_ss, a_rs.at[pair], ring(step))

    def first_copy(part, step):
        start = ((q + step) % 8) * ROWS + part * 16
        src = fields.at[local_plane(0), :, pl.ds(pl.multiple_of(start, 16), 16)]
        dst = own.at[0, half, slot, :, pl.ds(part * 16, 16)]
        if step == 0:
            return pltpu.make_async_copy(src, dst, a_rs.at[4 * part])
        return remote(src, dst, a_ss, a_rs.at[4 * part], ring(step))

    def momenta_copy(pair, step):
        src = slab.at[local_plane(pair), :, rows_of((q + step) % 8)]
        dst = mom.at[slot, 4 + half * 4 + local_plane(pair), :, inner]
        if step == 0:
            return pltpu.make_async_copy(src, dst, c_rs.at[pair])
        return remote(src, dst, c_ss, c_rs.at[pair], ring(step))

    def edge_copy(step):
        src, dst = edges.at[step], mom.at[slot, pl.ds(4 + half * 4, 4), :, beside_inner]
        if step == 0:
            return pltpu.make_async_copy(src, dst, ch_rs)
        return remote(src, dst, ch_ss, ch_rs, ring(step))

    def fill_edges():
        upper = lax.broadcasted_iota(jnp.int32, (2, 8, LANES), 1) < PAD
        for step in range(8):
            base = ((q + step) % 8) * ROWS
            after = pl.ds(pl.multiple_of((base + ROWS) % SIDE, 8), 8)
            ahead = pl.ds(pl.multiple_of((base + SIDE - 8) % SIDE, 8), 8)
            for plane in range(4):
                edges[step, plane] = jnp.where(upper, slab[plane, :, after, :], slab[plane, :, ahead, :])

    def flag_copy(step):
        if step == 0:
            return pltpu.make_async_copy(flag, flags.at[q], f_rs)
        return remote(flag, flags.at[q], f_ss, f_rs, ring(step))

    took(fields, here.at[0])
    for step in range(8):
        first_copy(0, step).start()
    for copy in small:
        copy.wait()
    flag[...] = jnp.full(flag.shape, accept[0], jnp.int32)

    alive = [[(counts[4 * ((y + d) % 4) + i] > 0).astype(jnp.int32) for i in range(4)] for d in range(4)]
    before = [[sum(alive[d][:i], jnp.int32(0)) for i in range(4)] for d in range(4)]
    total = [sum(alive[d], jnp.int32(0)) for d in range(4)]
    mine = [jnp.int32(-1)] * 4
    for c in range(4):
        for i in range(4):
            mine[c] = jnp.where((alive[0][i] == 1) & (before[0][i] == c), i, mine[c])
    split_up = jnp.minimum(total[3], 4 - total[2])
    split = jnp.minimum(total[2], 4 - total[1])
    cum, parent = jnp.int32(0), [jnp.int32(0)] * SLOTS
    for r in range(16):
        cum = cum + counts[r]
        for s in range(SLOTS):
            parent[s] = parent[s] + (cum <= 4 * y + s).astype(jnp.int32)
    code = []
    for s in range(SLOTS):
        value = jnp.int32(0)
        for d in range(4):
            for i in range(4):
                k = before[d][i]
                if d == 0:
                    way = jnp.int32(i)
                elif d == 1:
                    way = 4 + k
                elif d == 3:
                    way = 8 + k
                else:
                    way = jnp.where(k < split, 12 + total[1] + k, 16 + total[3] + k - split)
                value = jnp.where(parent[s] == 4 * ((y + d) % 4) + i, way, value)
        code.append(value)

    def same(value, number):
        return jnp.full((2, 8, LANES), value, jnp.int32) == number

    def octet(t):
        turn, late = t % 4, t >= 8
        pair = jnp.where(late, 2 + t // 2 % 2, t // 4)
        outer = jnp.where(late, t < 12, turn < 2)
        piece = jnp.where(outer, t % 2 * 3, 1 + t % 2)
        return pair, pl.ds(pl.multiple_of(jnp.where(pair == 0, turn, piece) * 8, 8), 8)

    def assemble(t, forward):
        pair, rows = octet(jnp.minimum(t, CHUNKS - 1))
        for c in range(4):
            own_here = [same(mine[c], i) for i in range(4)]
            down_here = [same(total[0], c - f) for f in range(c + 1)]
            up_here = [same(split_up + c - total[0], f) for f in range(4)]
            for h in range(2):
                pieces = [own[pair, h, i, :, rows, :] for i in range(4)]
                if forward:
                    down, up = from_above[t - LAG, 0, h], from_below[t - LAG, 0, h]
                    for f in range(1, c + 1):
                        down = jnp.where(down_here[f], from_above[t - LAG, f, h], down)
                    for f in range(1, 4):
                        up = jnp.where(up_here[f], from_below[t - LAG, f, h], up)
                else:
                    down = up = pieces[0]
                for i in range(4):
                    down = jnp.where(own_here[i], pieces[i], down)
                    up = jnp.where(own_here[i], pieces[i], up)
                send_down[t, c, h] = down
                send_up[t, c, h] = up

    def up_copy(t):
        return remote(send_up.at[t], from_below.at[t], up_ss, m_rs.at[t], above)

    def down_copy(t):
        return remote(send_down.at[t], from_above.at[t], down_ss, m_rs.at[t], below)

    def pick(u):
        pair, rows = octet(u)
        for s in range(SLOTS):
            here_ = [same(code[s], k) for k in range(20)]
            for h in range(2):
                value = own[pair, h, 0, :, rows, :]
                for i in range(1, 4):
                    value = jnp.where(here_[i], own[pair, h, i, :, rows, :], value)
                for c in range(4):
                    value = jnp.where(here_[4 + c], from_above[u, c, h], value)
                    value = jnp.where(here_[8 + c], from_below[u, c, h], value)
                    value = jnp.where(here_[12 + c], from_above[u + LAG, c, h], value)
                    value = jnp.where(here_[16 + c], from_below[u + LAG, c, h], value)
                plane = 4 + pair if h == 0 else 11 - pair
                phi0[s, plane, :, rows, :] = value

    def z_copies(pair):
        return (
            remote(phi0.at[:, 4 + pair], phi0.at[:, 12 + pair], z_ss, z_rs.at[pair], z_last),
            remote(phi0.at[:, 11 - pair], phi0.at[:, 3 - pair], z_ss, z_rs.at[pair], z_next),
        )

    zm_copies = (
        remote(mom.at[:, 4], mom.at[:, 12], zm_ss, zm_rs, z_last),
        remote(mom.at[:, 11], mom.at[:, 3], zm_ss, zm_rs, z_next),
    )

    def row_copies(pair):
        copies = []
        for n, plane in enumerate((4 + pair, 11 - pair)):
            copies.append(remote(phi0.at[:, plane, :, first], phi0.at[:, plane, :, high], r_ss, r_rs.at[pair], ring(-1)))
            copies.append(remote(phi0.at[:, plane, :, last], phi0.at[:, plane, :, low], r_ss, r_rs.at[pair], ring(1)))
        return copies

    momenta_pair = mom.at[:, pl.ds(4, 2), :, inner]
    row_halo = phi0.at[:, pl.ds(4, 2), :, beside_inner]

    def tick(t, carry):
        @pl.when(t == 0)
        def _():
            for step in range(8):
                first_copy(1, step).start()

        @pl.when((t < 5) & (t % 2 == 0))
        def _():
            for step in range(8):
                field_copy(t // 2 + 1, step).start()

        @pl.when((t == 0) | (t == 2))
        def _():
            took(own.at[0, :, :, :, pl.ds(0, 16)], a_rs.at[2 * t])

        @pl.when((t == 4) | (t == 8) | (t == 10))
        def _():
            pair = t // 4 + t // 10
            took(own.at[pair], a_rs.at[pair])

        @pl.when(t >= LAG)
        def _():
            took(own.at[0, 0], m_rs.at[t - LAG])

        @pl.when(t < LAG)
        def _():
            assemble(t, False)

        @pl.when((t >= LAG) & (t < MESSAGES))
        def _():
            assemble(t, True)

        @pl.when(t < MESSAGES)
        def _():
            up_copy(t).start()
            down_copy(t).start()

        @pl.when(t == 6)
        def _():
            took(slab, here.at[1])
            fill_edges()
            for step in range(8):
                edge_copy(step).start()
                flag_copy(step).start()

        @pl.when((t >= 8) & (t < 16) & (t % 2 == 0))
        def _():
            for step in range(8):
                momenta_copy((t - 8) // 2, step).start()

        @pl.when(t >= 2 * LAG)
        def _():
            pick(t - 2 * LAG)

        @pl.when((t == 2 * LAG + 3) | (t == 2 * LAG + 5) | (t == 2 * LAG + 9) | (t == 2 * LAG + 11))
        def _():
            for copy in row_copies((t - 2 * LAG - 1) // 3):
                copy.start()

        @pl.when((t == 2 * LAG + 5) | (t == 2 * LAG + 7))
        def _():
            pair = (t - 2 * LAG - 5) // 2
            took(row_halo, r_rs.at[pair])
            for copy in z_copies(pair):
                copy.start()

        @pl.when(t == 14)
        def _():
            took(mom.at[:, pl.ds(4, 8), :, beside_inner], ch_rs)
            took(momenta_pair, c_rs.at[0])
            for copy in zm_copies:
                copy.start()

        return carry

    lax.fori_loop(0, MESSAGES + LAG, tick, 0)

    for pair in range(1, PAIRS):
        took(momenta_pair, c_rs.at[pair])
    took(flags, f_rs)
    took(mom.at[:, pl.ds(0, 2)], zm_rs)
    took(mom.at[:, pl.ds(0, 2)], zm_ss)
    for pair in range(2):
        took(phi0.at[:, pl.ds(0, 2)], z_rs.at[pair])
    for pair in range(2, PAIRS):
        took(row_halo, r_rs.at[pair])

    def end_copies(k, s):
        src, n = (phi2, phi3)[k - 2].at[s], k - 2
        return (
            remote(src.at[0], sides.at[n, s, 1], d_ss, d_rs.at[n, s], z_last),
            remote(src.at[7], sides.at[n, s, 0], d_ss, d_rs.at[n, s], z_next),
        )

    PARTS = ((2, 2), (1, 1), (0, 1))

    def result_copy(s, h, part, away):
        first_plane, number = PARTS[part]
        src = done.at[s, pl.ds(8 - number - first_plane if h else first_plane, number)]
        dst = out.at[0, pl.ds(4 - number - first_plane if h else first_plane, number), rows_of(q)]
        if away:
            return remote(src, dst, e_ss, e_rs, place(4 * h + s, y, z))
        return pltpu.make_async_copy(src, dst, e_rs)

    def results(s, part):
        for h in range(2):
            @pl.when(q == 4 * h + s)
            def _():
                result_copy(s, h, part, False).start()

            @pl.when(q != 4 * h + s)
            def _():
                result_copy(s, h, part, True).start()

    tiles = range(ALL // 8)

    def spread(t):
        return pl.ds(t, 8, stride=ALL // 8)

    edge_lane = lax.broadcasted_iota(jnp.int32, (8, LANES), 1)
    first_lane, last_lane = edge_lane == 0, edge_lane == LANES - 1

    def natural(ref, plane):
        return [[ref[plane, n, spread(t), :] for t in tiles] for n in range(2)]

    def packed(ref, plane):
        return [[ref[plane, n, 8 * t:8 * t + 8, :] for t in tiles] for n in range(2)]

    def keep(ref, plane, values):
        for n in range(2):
            for t in tiles:
                ref[plane, n, 8 * t:8 * t + 8, :] = values[n][t]

    def each(act, *args):
        return [[act(*(arg[n][t] for arg in args)) for t in tiles] for n in range(2)]

    def kick(below_, centre, above_, scale):
        back = [[pltpu.roll(centre[n][t], 1, 1) for t in tiles] for n in range(2)]
        fore = [[pltpu.roll(centre[n][t], LANES - 1, 1) for t in tiles] for n in range(2)]
        result = [[], []]
        for n in range(2):
            for t in tiles:
                c = centre[n][t]
                ahead = centre[n][t - 1] if t > 0 else pltpu.roll(centre[n][-1], 1, 0)
                after = centre[n][t + 1] if t < len(tiles) - 1 else pltpu.roll(centre[n][0], 7, 0)
                left_ = jnp.where(first_lane, back[1 - n][t], back[n][t])
                right_ = jnp.where(last_lane, fore[1 - n][t], fore[n][t])
                beside = (below_[n][t] + above_[n][t]) + (ahead + after) + (left_ + right_)
                result[n].append((scale * 2.0 * KAPPA) * beside + c * (scale * (4.0 * LAMBDA - 2.0) - (scale * 4.0 * LAMBDA) * (c * c)))
        return result

    def finish(s, taken, plane, trio, move):
        push = kick(*trio, EPS * EPS)
        start = natural(phi0.at[s], 4 + plane)
        value = each(lambda c, m, f, b: jnp.where(taken, c + (m + f), b), trio[1], move, push, start)
        for n in range(2):
            for t in tiles:
                turned[plane, n, spread(t), :] = value[n][t]
            done[s, plane, :, n * LANES:(n + 1) * LANES] = turned[plane, n, :ROWS, :]

    def advance(trio, move, scale=EPS * EPS):
        push = kick(*trio, scale)
        move = each(lambda m, f: m + f, move, push)
        return move, each(lambda c, m: c + m, trio[1], move)

    def one_slot(n, carry):
        s = (n % 2) * 2 + n // 2
        taken = flags[s] == 1
        start, second, third, held = phi0.at[s], phi2.at[s], phi3.at[s], moves.at[s]
        trio = [None, natural(start, 2), natural(start, 3)]
        for plane in range(3, 13):
            trio = trio[1:] + [natural(start, plane + 1)]
            move = each(lambda m: EPS * m, natural(mom.at[s], plane))
            move, value = advance(trio, move, 0.5 * EPS * EPS)
            if 4 <= plane < 12:
                keep(held, plane - 4, move)
            keep(phi1, plane - 3, value)
        trio = [None, packed(phi1, 0), packed(phi1, 1)]
        for plane in range(8):
            trio = trio[1:] + [packed(phi1, plane + 2)]
            move, value = advance(trio, packed(held, plane))
            keep(held, plane, move)
            keep(second, plane, value)
        for copy in end_copies(2, s):
            copy.start()
        trio = [None, packed(second, 0), packed(second, 1)]
        for plane in range(1, 7):
            trio = trio[1:] + [packed(second, plane + 1)]
            move, value = advance(trio, packed(held, plane))
            keep(held, plane, move)
            keep(third, plane, value)
        trio = [None, packed(third, 1), packed(third, 2)]
        for plane in range(2, 6):
            trio = trio[1:] + [packed(third, plane + 1)]
            finish(s, taken, plane, trio, packed(held, plane))
        results(s, 0)
        return carry

    def next_planes(n, carry):
        s = (n % 2) * 2 + n // 2
        taken = flags[s] == 1
        second, third, held, beyond = phi2.at[s], phi3.at[s], moves.at[s], sides.at[0, s]
        took(sides.at[0, s], d_rs.at[0, s])
        for plane in (0, 7):
            inside = packed(second, 1 if plane == 0 else 6)
            move, value = advance([packed(beyond, plane // 7), packed(second, plane), inside], packed(held, plane))
            keep(held, plane, move)
            keep(third, plane, value)
        for copy in end_copies(3, s):
            copy.start()
        for plane in (1, 6):
            finish(s, taken, plane, [packed(third, plane + n_) for n_ in (-1, 0, 1)], packed(held, plane))
        results(s, 1)
        return carry

    def end_planes(n, carry):
        s = (n % 2) * 2 + n // 2
        taken = flags[s] == 1
        third, held, beyond = phi3.at[s], moves.at[s], sides.at[1, s]
        took(sides.at[1, s], d_rs.at[1, s])
        for plane in (0, 7):
            inside = packed(third, 1 if plane == 0 else 6)
            finish(s, taken, plane, [packed(beyond, plane // 7), packed(third, plane), inside], packed(held, plane))
        results(s, 2)
        return carry

    lax.fori_loop(0, SLOTS, one_slot, 0)
    lax.fori_loop(0, SLOTS, next_planes, 0)
    lax.fori_loop(0, SLOTS, end_planes, 0)

    seven = pl.ds(0, 7 * ROWS)
    took(fields.at[:, :, seven], a_ss)
    took(slab.at[:, :, seven], c_ss)
    took(edges.at[pl.ds(0, 7)], ch_ss)
    took(flags.at[pl.ds(0, 7)], f_ss)
    took(send_up, up_ss)
    took(send_down, down_ss)
    took(phi0.at[:, pl.ds(0, 4)], z_ss)
    took(phi0.at[:, pl.ds(4, 8), :, beside_inner], r_ss)
    took(sides, d_ss)
    took(out.at[0, :, seven], e_ss)
    took(out, e_rs)


def local(field, momenta, counts, accept):
    f32, dma = jnp.float32, pltpu.SemaphoreType.DMA
    message = (MESSAGES, 4, 2, 2, 8, LANES)
    plane = (2, ALL, LANES)
    return pl.pallas_call(
        kernel,
        out_shape=jax.ShapeDtypeStruct(field.shape, f32),
        in_specs=[
            pl.BlockSpec(memory_space=pltpu.HBM),
            pl.BlockSpec(memory_space=pltpu.HBM),
            pl.BlockSpec(memory_space=pl.ANY),
            pl.BlockSpec(memory_space=pl.ANY),
        ],
        out_specs=pl.BlockSpec(memory_space=pltpu.VMEM),
        scratch_shapes=[
            pltpu.VMEM((PAIRS, 2, SLOTS, 2, ROWS, LANES), f32),
            pltpu.VMEM(message, f32),
            pltpu.VMEM(message, f32),
            pltpu.VMEM(message, f32),
            pltpu.VMEM(message, f32),
            pltpu.VMEM((SLOTS, 16) + plane, f32),
            pltpu.VMEM((10,) + plane, f32),
            pltpu.VMEM((SLOTS, 8) + plane, f32),
            pltpu.VMEM((SLOTS, 8) + plane, f32),
            pltpu.VMEM((SLOTS, 16) + plane, f32),
            pltpu.VMEM((SLOTS, 8) + plane, f32),
            pltpu.VMEM((2, SLOTS, 2) + plane, f32),
            pltpu.VMEM((SLOTS, 8, ROWS, SIDE), f32),
            pltpu.VMEM((8,) + plane, f32),
            pltpu.VMEM((4, 2, SIDE, LANES), f32),
            pltpu.VMEM((4, 2, SIDE, LANES), f32),
            pltpu.VMEM((8, 4, 2, 8, LANES), f32),
            pltpu.VMEM((8, LANES), jnp.int32),
            pltpu.VMEM((8, 8, LANES), jnp.int32),
            dma, dma((PAIRS + 1,)), dma, dma((PAIRS,)), dma, dma, dma, dma,
            dma, dma, dma((MESSAGES,)),
            dma, dma((2,)), dma, dma,
            dma, dma((PAIRS,)), dma, dma((2, SLOTS)), dma, dma, dma((4,)),
            pltpu.SMEM((16,), jnp.int32),
            pltpu.SMEM((1,), jnp.int32),
        ],
        compiler_params=pltpu.CompilerParams(collective_id=0, has_side_effects=True, vmem_limit_bytes=52 * 1024 * 1024),
    )(field, momenta, counts, accept)


def solution(mesh):
    placed = (P("rep", "gz", None, None), P("rep", "gz", None, None), P(), P("rep"))
    return jax.shard_map(
        local, mesh=mesh, in_specs=placed, out_specs=P("rep", "gz", None, None), check_vma=False
    )
```

```python
import jax
import jax.numpy as jnp
from jax import lax
from jax.experimental import pallas as pl
from jax.experimental.pallas import tpu as pltpu
from jax.sharding import PartitionSpec as P

KAPPA = 0.16
LAMBDA = 0.015
EPS = 0.75

MESH = pl.DeviceIdType.MESH
SLOTS = 4
ROWS = 32
PAD = 4
ALL = ROWS + 2 * PAD
SIDE = 256
LANES = 128
PAIRS = 4
CHUNKS = 16
LAG = 3
MESSAGES = CHUNKS + LAG


def kernel(field, momenta, counts_in, accept_in, out, own, send_up, send_down, from_below, from_above, phi0, phi1, phi2, phi3, mom, moves, sides,
           done, turned, fields, slab, edges, flag, flags, a_ss, a_rs, c_ss, c_rs, ch_ss, ch_rs, f_ss, f_rs, up_ss, down_ss, m_rs, z_ss, z_rs, zm_ss, zm_rs,
           r_ss, r_rs, d_ss, d_rs, e_ss, e_rs, here, counts, accept):
    rep, gz = lax.axis_index("rep"), lax.axis_index("gz")
    y, z = rep // 4, gz // 2
    q = (gz % 2) * 4 + rep % 4
    slot, half = rep % 4, gz % 2

    inner = pl.ds(0, ROWS)
    first, last = pl.ds(0, PAD), pl.ds(ROWS - PAD, PAD)
    high, low = pl.ds(ROWS, PAD), pl.ds(ROWS + PAD, PAD)
    beside_inner = pl.ds(ROWS, 2 * PAD)

    def place(ring, row, depth):
        return (row * 4 + ring % 4, depth * 2 + ring // 4)

    def ring(step):
        return place((q + step + 8) % 8, y, z)

    above, below = place(q, (y + 1) % 4, z), place(q, (y + 3) % 4, z)
    z_next, z_last = place(q, y, (z + 1) % 8), place(q, y, (z + 7) % 8)

    def remote(src, dst, ss, rs, device):
        return pltpu.make_async_remote_copy(src_ref=src, dst_ref=dst, send_sem=ss, recv_sem=rs, device_id=device, device_id_type=MESH)

    def took(like, sem):
        pltpu.make_async_copy(like, like, sem).wait()

    small = (pltpu.make_async_copy(counts_in, counts, here.at[2]), pltpu.make_async_copy(accept_in, accept, here.at[3]))
    for copy in small:
        copy.start()
    for n, (src, dst) in enumerate(((field, fields), (momenta, slab))):
        for side in range(2):
            pltpu.make_async_copy(src.at[0, :, :, pl.ds(side * LANES, LANES)], dst.at[:, side], here.at[n]).start()

    barrier = pltpu.get_barrier_semaphore()
    partners = [ring(step) for step in range(1, 8)] + [above, below, z_next, z_last]
    for device in partners:
        pl.semaphore_signal(barrier, inc=1, device_id=device, device_id_type=MESH)
    pl.semaphore_wait(barrier, len(partners))

    def rows_of(place_):
        return pl.ds(pl.multiple_of(place_ * ROWS, ROWS), ROWS)

    def local_plane(pair):
        return pair + half * (3 - 2 * pair)

    def field_copy(pair, step):
        src = fields.at[local_plane(pair), :, rows_of((q + step) % 8)]
        dst = own.at[pair, half, slot]
        if step == 0:
            return pltpu.make_async_copy(src, dst, a_rs.at[pair])
        return remote(src, dst, a_ss, a_rs.at[pair], ring(step))

    def first_copy(part, step):
        start = ((q + step) % 8) * ROWS + part * 16
        src = fields.at[local_plane(0), :, pl.ds(pl.multiple_of(start, 16), 16)]
        dst = own.at[0, half, slot, :, pl.ds(part * 16, 16)]
        if step == 0:
            return pltpu.make_async_copy(src, dst, a_rs.at[4 * part])
        return remote(src, dst, a_ss, a_rs.at[4 * part], ring(step))

    def momenta_copy(pair, step):
        src = slab.at[local_plane(pair), :, rows_of((q + step) % 8)]
        dst = mom.at[slot, 4 + half * 4 + local_plane(pair), :, inner]
        if step == 0:
            return pltpu.make_async_copy(src, dst, c_rs.at[pair])
        return remote(src, dst, c_ss, c_rs.at[pair], ring(step))

    def edge_copy(step):
        src, dst = edges.at[step], mom.at[slot, pl.ds(4 + half * 4, 4), :, beside_inner]
        if step == 0:
            return pltpu.make_async_copy(src, dst, ch_rs)
        return remote(src, dst, ch_ss, ch_rs, ring(step))

    def fill_edges():
        upper = lax.broadcasted_iota(jnp.int32, (2, 8, LANES), 1) < PAD
        for step in range(8):
            base = ((q + step) % 8) * ROWS
            after = pl.ds(pl.multiple_of((base + ROWS) % SIDE, 8), 8)
            ahead = pl.ds(pl.multiple_of((base + SIDE - 8) % SIDE, 8), 8)
            for plane in range(4):
                edges[step, plane] = jnp.where(upper, slab[plane, :, after, :], slab[plane, :, ahead, :])

    def flag_copy(step):
        if step == 0:
            return pltpu.make_async_copy(flag, flags.at[q], f_rs)
        return remote(flag, flags.at[q], f_ss, f_rs, ring(step))

    took(fields, here.at[0])
    for step in range(8):
        first_copy(0, step).start()
    for copy in small:
        copy.wait()
    flag[...] = jnp.full(flag.shape, accept[0], jnp.int32)

    alive = [[(counts[4 * ((y + d) % 4) + i] > 0).astype(jnp.int32) for i in range(4)] for d in range(4)]
    before = [[sum(alive[d][:i], jnp.int32(0)) for i in range(4)] for d in range(4)]
    total = [sum(alive[d], jnp.int32(0)) for d in range(4)]
    mine = [jnp.int32(-1)] * 4
    for c in range(4):
        for i in range(4):
            mine[c] = jnp.where((alive[0][i] == 1) & (before[0][i] == c), i, mine[c])
    split_up = jnp.minimum(total[3], 4 - total[2])
    split = jnp.minimum(total[2], 4 - total[1])
    cum, parent = jnp.int32(0), [jnp.int32(0)] * SLOTS
    for r in range(16):
        cum = cum + counts[r]
        for s in range(SLOTS):
            parent[s] = parent[s] + (cum <= 4 * y + s).astype(jnp.int32)
    code = []
    for s in range(SLOTS):
        value = jnp.int32(0)
        for d in range(4):
            for i in range(4):
                k = before[d][i]
                if d == 0:
                    way = jnp.int32(i)
                elif d == 1:
                    way = 4 + k
                elif d == 3:
                    way = 8 + k
                else:
                    way = jnp.where(k < split, 12 + total[1] + k, 16 + total[3] + k - split)
                value = jnp.where(parent[s] == 4 * ((y + d) % 4) + i, way, value)
        code.append(value)

    def same(value, number):
        return jnp.full((2, 8, LANES), value, jnp.int32) == number

    def octet(t):
        turn, late = t % 4, t >= 8
        pair = jnp.where(late, 2 + t // 2 % 2, t // 4)
        outer = jnp.where(late, t < 12, turn < 2)
        piece = jnp.where(outer, t % 2 * 3, 1 + t % 2)
        return pair, pl.ds(pl.multiple_of(jnp.where(pair == 0, turn, piece) * 8, 8), 8)

    def assemble(t, forward):
        pair, rows = octet(jnp.minimum(t, CHUNKS - 1))
        for c in range(4):
            own_here = [same(mine[c], i) for i in range(4)]
            down_here = [same(total[0], c - f) for f in range(c + 1)]
            up_here = [same(split_up + c - total[0], f) for f in range(4)]
            for h in range(2):
                pieces = [own[pair, h, i, :, rows, :] for i in range(4)]
                if forward:
                    down, up = from_above[t - LAG, 0, h], from_below[t - LAG, 0, h]
                    for f in range(1, c + 1):
                        down = jnp.where(down_here[f], from_above[t - LAG, f, h], down)
                    for f in range(1, 4):
                        up = jnp.where(up_here[f], from_below[t - LAG, f, h], up)
                else:
                    down = up = pieces[0]
                for i in range(4):
                    down = jnp.where(own_here[i], pieces[i], down)
                    up = jnp.where(own_here[i], pieces[i], up)
                send_down[t, c, h] = down
                send_up[t, c, h] = up

    def up_copy(t):
        return remote(send_up.at[t], from_below.at[t], up_ss, m_rs.at[t], above)

    def down_copy(t):
        return remote(send_down.at[t], from_above.at[t], down_ss, m_rs.at[t], below)

    def pick(u):
        pair, rows = octet(u)
        for s in range(SLOTS):
            here_ = [same(code[s], k) for k in range(20)]
            for h in range(2):
                value = own[pair, h, 0, :, rows, :]
                for i in range(1, 4):
                    value = jnp.where(here_[i], own[pair, h, i, :, rows, :], value)
                for c in range(4):
                    value = jnp.where(here_[4 + c], from_above[u, c, h], value)
                    value = jnp.where(here_[8 + c], from_below[u, c, h], value)
                    value = jnp.where(here_[12 + c], from_above[u + LAG, c, h], value)
                    value = jnp.where(here_[16 + c], from_below[u + LAG, c, h], value)
                plane = 4 + pair if h == 0 else 11 - pair
                phi0[s, plane, :, rows, :] = value

    def z_copies(pair):
        return (
            remote(phi0.at[:, 4 + pair], phi0.at[:, 12 + pair], z_ss, z_rs.at[pair], z_last),
            remote(phi0.at[:, 11 - pair], phi0.at[:, 3 - pair], z_ss, z_rs.at[pair], z_next),
        )

    zm_copies = (
        remote(mom.at[:, 4], mom.at[:, 12], zm_ss, zm_rs, z_last),
        remote(mom.at[:, 11], mom.at[:, 3], zm_ss, zm_rs, z_next),
    )

    def row_copies(pair):
        copies = []
        for n, plane in enumerate((4 + pair, 11 - pair)):
            copies.append(remote(phi0.at[:, plane, :, first], phi0.at[:, plane, :, high], r_ss, r_rs.at[pair], ring(-1)))
            copies.append(remote(phi0.at[:, plane, :, last], phi0.at[:, plane, :, low], r_ss, r_rs.at[pair], ring(1)))
        return copies

    momenta_pair = mom.at[:, pl.ds(4, 2), :, inner]
    row_halo = phi0.at[:, pl.ds(4, 2), :, beside_inner]

    def tick(t, carry):
        @pl.when(t == 0)
        def _():
            for step in range(8):
                first_copy(1, step).start()

        @pl.when((t < 5) & (t % 2 == 0))
        def _():
            for step in range(8):
                field_copy(t // 2 + 1, step).start()

        @pl.when((t == 0) | (t == 2))
        def _():
            took(own.at[0, :, :, :, pl.ds(0, 16)], a_rs.at[2 * t])

        @pl.when((t == 4) | (t == 8) | (t == 10))
        def _():
            pair = t // 4 + t // 10
            took(own.at[pair], a_rs.at[pair])

        @pl.when(t >= LAG)
        def _():
            took(own.at[0, 0], m_rs.at[t - LAG])

        @pl.when(t < LAG)
        def _():
            assemble(t, False)

        @pl.when((t >= LAG) & (t < MESSAGES))
        def _():
            assemble(t, True)

        @pl.when(t < MESSAGES)
        def _():
            up_copy(t).start()
            down_copy(t).start()

        @pl.when(t == 6)
        def _():
            took(slab, here.at[1])
            fill_edges()
            for step in range(8):
                edge_copy(step).start()
                flag_copy(step).start()

        @pl.when((t >= 8) & (t < 16) & (t % 2 == 0))
        def _():
            for step in range(8):
                momenta_copy((t - 8) // 2, step).start()

        @pl.when(t >= 2 * LAG)
        def _():
            pick(t - 2 * LAG)

        @pl.when((t == 2 * LAG + 3) | (t == 2 * LAG + 5) | (t == 2 * LAG + 9) | (t == 2 * LAG + 11))
        def _():
            for copy in row_copies((t - 2 * LAG - 1) // 3):
                copy.start()

        @pl.when((t == 2 * LAG + 5) | (t == 2 * LAG + 7))
        def _():
            pair = (t - 2 * LAG - 5) // 2
            took(row_halo, r_rs.at[pair])
            for copy in z_copies(pair):
                copy.start()

        @pl.when(t == 14)
        def _():
            took(mom.at[:, pl.ds(4, 8), :, beside_inner], ch_rs)
            took(momenta_pair, c_rs.at[0])
            for copy in zm_copies:
                copy.start()

        return carry

    lax.fori_loop(0, MESSAGES + LAG, tick, 0)

    for pair in range(1, PAIRS):
        took(momenta_pair, c_rs.at[pair])
    took(flags, f_rs)
    took(mom.at[:, pl.ds(0, 2)], zm_rs)
    took(mom.at[:, pl.ds(0, 2)], zm_ss)
    for pair in range(2):
        took(phi0.at[:, pl.ds(0, 2)], z_rs.at[pair])
    for pair in range(2, PAIRS):
        took(row_halo, r_rs.at[pair])

    def end_copies(k, s):
        src, n = (phi2, phi3)[k - 2].at[s], k - 2
        return (
            remote(src.at[0], sides.at[n, s, 1], d_ss, d_rs.at[n, s], z_last),
            remote(src.at[7], sides.at[n, s, 0], d_ss, d_rs.at[n, s], z_next),
        )

    PARTS = ((2, 2), (1, 1), (0, 1))

    def result_copy(s, h, part, away):
        first_plane, number = PARTS[part]
        src = done.at[s, pl.ds(8 - number - first_plane if h else first_plane, number)]
        dst = out.at[0, pl.ds(4 - number - first_plane if h else first_plane, number), rows_of(q)]
        if away:
            return remote(src, dst, e_ss, e_rs, place(4 * h + s, y, z))
        return pltpu.make_async_copy(src, dst, e_rs)

    def results(s, part):
        for h in range(2):
            @pl.when(q == 4 * h + s)
            def _():
                result_copy(s, h, part, False).start()

            @pl.when(q != 4 * h + s)
            def _():
                result_copy(s, h, part, True).start()

    tiles = range(ALL // 8)

    def spread(t):
        return pl.ds(t, 8, stride=ALL // 8)

    edge_lane = lax.broadcasted_iota(jnp.int32, (8, LANES), 1)
    first_lane, last_lane = edge_lane == 0, edge_lane == LANES - 1

    def natural(ref, plane):
        return [[ref[plane, n, spread(t), :] for t in tiles] for n in range(2)]

    def packed(ref, plane):
        return [[ref[plane, n, 8 * t:8 * t + 8, :] for t in tiles] for n in range(2)]

    def keep(ref, plane, values):
        for n in range(2):
            for t in tiles:
                ref[plane, n, 8 * t:8 * t + 8, :] = values[n][t]

    def each(act, *args):
        return [[act(*(arg[n][t] for arg in args)) for t in tiles] for n in range(2)]

    def kick(below_, centre, above_, scale):
        back = [[pltpu.roll(centre[n][t], 1, 1) for t in tiles] for n in range(2)]
        fore = [[pltpu.roll(centre[n][t], LANES - 1, 1) for t in tiles] for n in range(2)]
        result = [[], []]
        for n in range(2):
            for t in tiles:
                c = centre[n][t]
                ahead = centre[n][t - 1] if t > 0 else pltpu.roll(centre[n][-1], 1, 0)
                after = centre[n][t + 1] if t < len(tiles) - 1 else pltpu.roll(centre[n][0], 7, 0)
                left_ = jnp.where(first_lane, back[1 - n][t], back[n][t])
                right_ = jnp.where(last_lane, fore[1 - n][t], fore[n][t])
                beside = (below_[n][t] + above_[n][t]) + (ahead + after) + (left_ + right_)
                result[n].append((scale * 2.0 * KAPPA) * beside + c * (scale * (4.0 * LAMBDA - 2.0) - (scale * 4.0 * LAMBDA) * (c * c)))
        return result

    def finish(s, taken, plane, trio, move):
        push = kick(*trio, EPS * EPS)
        start = natural(phi0.at[s], 4 + plane)
        value = each(lambda c, m, f, b: jnp.where(taken, c + (m + f), b), trio[1], move, push, start)
        for n in range(2):
            for t in tiles:
                turned[plane, n, spread(t), :] = value[n][t]
            done[s, plane, :, n * LANES:(n + 1) * LANES] = turned[plane, n, :ROWS, :]

    def advance(trio, move, scale=EPS * EPS):
        push = kick(*trio, scale)
        move = each(lambda m, f: m + f, move, push)
        return move, each(lambda c, m: c + m, trio[1], move)

    def opening(n, carry):
        s = (n % 2) * 2 + n // 2
        start, second, held = phi0.at[s], phi2.at[s], moves.at[s]
        trio = [None, natural(start, 2), natural(start, 3)]
        for plane in range(3, 13):
            trio = trio[1:] + [natural(start, plane + 1)]
            move = each(lambda m: EPS * m, natural(mom.at[s], plane))
            move, value = advance(trio, move, 0.5 * EPS * EPS)
            if 4 <= plane < 12:
                keep(held, plane - 4, move)
            keep(phi1, plane - 3, value)
        trio = [None, packed(phi1, 0), packed(phi1, 1)]
        for plane in range(8):
            trio = trio[1:] + [packed(phi1, plane + 2)]
            move, value = advance(trio, packed(held, plane))
            keep(held, plane, move)
            keep(second, plane, value)
        for copy in end_copies(2, s):
            copy.start()
        return carry

    def inner_planes(n, carry):
        s = (n % 2) * 2 + n // 2
        taken = flags[s] == 1
        second, third, held = phi2.at[s], phi3.at[s], moves.at[s]
        trio = [None, packed(second, 0), packed(second, 1)]
        for plane in range(1, 7):
            trio = trio[1:] + [packed(second, plane + 1)]
            move, value = advance(trio, packed(held, plane))
            keep(held, plane, move)
            keep(third, plane, value)
        trio = [None, packed(third, 1), packed(third, 2)]
        for plane in range(2, 6):
            trio = trio[1:] + [packed(third, plane + 1)]
            finish(s, taken, plane, trio, packed(held, plane))
        results(s, 0)
        return carry

    def next_planes(n, carry):
        s = (n % 2) * 2 + n // 2
        taken = flags[s] == 1
        second, third, held, beyond = phi2.at[s], phi3.at[s], moves.at[s], sides.at[0, s]
        took(sides.at[0, s], d_rs.at[0, s])
        for plane in (0, 7):
            inside = packed(second, 1 if plane == 0 else 6)
            move, value = advance([packed(beyond, plane // 7), packed(second, plane), inside], packed(held, plane))
            keep(held, plane, move)
            keep(third, plane, value)
        for copy in end_copies(3, s):
            copy.start()
        for plane in (1, 6):
            finish(s, taken, plane, [packed(third, plane + n_) for n_ in (-1, 0, 1)], packed(held, plane))
        results(s, 1)
        return carry

    def end_planes(n, carry):
        s = (n % 2) * 2 + n // 2
        taken = flags[s] == 1
        third, held, beyond = phi3.at[s], moves.at[s], sides.at[1, s]
        took(sides.at[1, s], d_rs.at[1, s])
        for plane in (0, 7):
            inside = packed(third, 1 if plane == 0 else 6)
            finish(s, taken, plane, [packed(beyond, plane // 7), packed(third, plane), inside], packed(held, plane))
        results(s, 2)
        return carry

    for some in ((0, 1), (1, SLOTS)):
        lax.fori_loop(*some, opening, 0)
        lax.fori_loop(*some, inner_planes, 0)
    lax.fori_loop(0, SLOTS, next_planes, 0)
    lax.fori_loop(0, SLOTS, end_planes, 0)

    seven = pl.ds(0, 7 * ROWS)
    took(fields.at[:, :, seven], a_ss)
    took(slab.at[:, :, seven], c_ss)
    took(edges.at[pl.ds(0, 7)], ch_ss)
    took(flags.at[pl.ds(0, 7)], f_ss)
    took(send_up, up_ss)
    took(send_down, down_ss)
    took(phi0.at[:, pl.ds(0, 4)], z_ss)
    took(phi0.at[:, pl.ds(4, 8), :, beside_inner], r_ss)
    took(sides, d_ss)
    took(out.at[0, :, seven], e_ss)
    took(out, e_rs)


def local(field, momenta, counts, accept):
    f32, dma = jnp.float32, pltpu.SemaphoreType.DMA
    message = (MESSAGES, 4, 2, 2, 8, LANES)
    plane = (2, ALL, LANES)
    return pl.pallas_call(
        kernel,
        out_shape=jax.ShapeDtypeStruct(field.shape, f32),
        in_specs=[
            pl.BlockSpec(memory_space=pltpu.HBM),
            pl.BlockSpec(memory_space=pltpu.HBM),
            pl.BlockSpec(memory_space=pl.ANY),
            pl.BlockSpec(memory_space=pl.ANY),
        ],
        out_specs=pl.BlockSpec(memory_space=pltpu.VMEM),
        scratch_shapes=[
            pltpu.VMEM((PAIRS, 2, SLOTS, 2, ROWS, LANES), f32),
            pltpu.VMEM(message, f32),
            pltpu.VMEM(message, f32),
            pltpu.VMEM(message, f32),
            pltpu.VMEM(message, f32),
            pltpu.VMEM((SLOTS, 16) + plane, f32),
            pltpu.VMEM((10,) + plane, f32),
            pltpu.VMEM((SLOTS, 8) + plane, f32),
            pltpu.VMEM((SLOTS, 8) + plane, f32),
            pltpu.VMEM((SLOTS, 16) + plane, f32),
            pltpu.VMEM((SLOTS, 8) + plane, f32),
            pltpu.VMEM((2, SLOTS, 2) + plane, f32),
            pltpu.VMEM((SLOTS, 8, ROWS, SIDE), f32),
            pltpu.VMEM((8,) + plane, f32),
            pltpu.VMEM((4, 2, SIDE, LANES), f32),
            pltpu.VMEM((4, 2, SIDE, LANES), f32),
            pltpu.VMEM((8, 4, 2, 8, LANES), f32),
            pltpu.VMEM((8, LANES), jnp.int32),
            pltpu.VMEM((8, 8, LANES), jnp.int32),
            dma, dma((PAIRS + 1,)), dma, dma((PAIRS,)), dma, dma, dma, dma,
            dma, dma, dma((MESSAGES,)),
            dma, dma((2,)), dma, dma,
            dma, dma((PAIRS,)), dma, dma((2, SLOTS)), dma, dma, dma((4,)),
            pltpu.SMEM((16,), jnp.int32),
            pltpu.SMEM((1,), jnp.int32),
        ],
        compiler_params=pltpu.CompilerParams(collective_id=0, has_side_effects=True, vmem_limit_bytes=52 * 1024 * 1024),
    )(field, momenta, counts, accept)


def solution(mesh):
    placed = (P("rep", "gz", None, None), P("rep", "gz", None, None), P(), P("rep"))
    return jax.shard_map(
        local, mesh=mesh, in_specs=placed, out_specs=P("rep", "gz", None, None), check_vma=False
    )
```

```python
import jax
import jax.numpy as jnp
from jax import lax
from jax.experimental import pallas as pl
from jax.experimental.pallas import tpu as pltpu
from jax.sharding import PartitionSpec as P

KAPPA = 0.16
LAMBDA = 0.015
EPS = 0.75

MESH = pl.DeviceIdType.MESH
SLOTS = 4
ROWS = 32
PAD = 4
ALL = ROWS + 2 * PAD
SIDE = 256
LANES = 128
PAIRS = 4
CHUNKS = 16
LAG = 3
MESSAGES = CHUNKS + LAG


def kernel(field, momenta, counts_in, accept_in, out, own, send_up, send_down, from_below, from_above, phi0, phi1, phi2, phi3, mom, moves, sides,
           done, turned, fields, slab, edges, flag, flags, a_ss, a_rs, c_ss, c_rs, ch_ss, ch_rs, f_ss, f_rs, up_ss, down_ss, m_rs, z_ss, z_rs, zm_ss, zm_rs,
           r_ss, r_rs, d_ss, d_rs, e_ss, e_rs, here, counts, accept):
    rep, gz = lax.axis_index("rep"), lax.axis_index("gz")
    y, z = rep // 4, gz // 2
    q = (gz % 2) * 4 + rep % 4
    slot, half = rep % 4, gz % 2

    inner = pl.ds(0, ROWS)
    first, last = pl.ds(0, PAD), pl.ds(ROWS - PAD, PAD)
    high, low = pl.ds(ROWS, PAD), pl.ds(ROWS + PAD, PAD)
    beside_inner = pl.ds(ROWS, 2 * PAD)

    def place(ring, row, depth):
        return (row * 4 + ring % 4, depth * 2 + ring // 4)

    def ring(step):
        return place((q + step + 8) % 8, y, z)

    above, below = place(q, (y + 1) % 4, z), place(q, (y + 3) % 4, z)
    z_next, z_last = place(q, y, (z + 1) % 8), place(q, y, (z + 7) % 8)

    def remote(src, dst, ss, rs, device):
        return pltpu.make_async_remote_copy(src_ref=src, dst_ref=dst, send_sem=ss, recv_sem=rs, device_id=device, device_id_type=MESH)

    def took(like, sem):
        pltpu.make_async_copy(like, like, sem).wait()

    small = (pltpu.make_async_copy(counts_in, counts, here.at[2]), pltpu.make_async_copy(accept_in, accept, here.at[3]))
    for copy in small:
        copy.start()
    for n, (src, dst) in enumerate(((field, fields), (momenta, slab))):
        for side in range(2):
            pltpu.make_async_copy(src.at[0, :, :, pl.ds(side * LANES, LANES)], dst.at[:, side], here.at[n]).start()

    barrier = pltpu.get_barrier_semaphore()
    partners = [ring(step) for step in range(1, 8)] + [above, below, z_next, z_last]
    for device in partners:
        pl.semaphore_signal(barrier, inc=1, device_id=device, device_id_type=MESH)
    pl.semaphore_wait(barrier, len(partners))

    def rows_of(place_):
        return pl.ds(pl.multiple_of(place_ * ROWS, ROWS), ROWS)

    def local_plane(pair):
        return pair + half * (3 - 2 * pair)

    def field_copy(pair, step):
        src = fields.at[local_plane(pair), :, rows_of((q + step) % 8)]
        dst = own.at[pair, half, slot]
        if step == 0:
            return pltpu.make_async_copy(src, dst, a_rs.at[pair])
        return remote(src, dst, a_ss, a_rs.at[pair], ring(step))

    def first_copy(part, step):
        start = ((q + step) % 8) * ROWS + part * 16
        src = fields.at[local_plane(0), :, pl.ds(pl.multiple_of(start, 16), 16)]
        dst = own.at[0, half, slot, :, pl.ds(part * 16, 16)]
        if step == 0:
            return pltpu.make_async_copy(src, dst, a_rs.at[4 * part])
        return remote(src, dst, a_ss, a_rs.at[4 * part], ring(step))

    def momenta_copy(pair, step):
        src = slab.at[local_plane(pair), :, rows_of((q + step) % 8)]
        dst = mom.at[slot, 4 + half * 4 + local_plane(pair), :, inner]
        if step == 0:
            return pltpu.make_async_copy(src, dst, c_rs.at[pair])
        return remote(src, dst, c_ss, c_rs.at[pair], ring(step))

    def edge_copy(step):
        src, dst = edges.at[step], mom.at[slot, pl.ds(4 + half * 4, 4), :, beside_inner]
        if step == 0:
            return pltpu.make_async_copy(src, dst, ch_rs)
        return remote(src, dst, ch_ss, ch_rs, ring(step))

    def fill_edges():
        upper = lax.broadcasted_iota(jnp.int32, (2, 8, LANES), 1) < PAD
        for step in range(8):
            base = ((q + step) % 8) * ROWS
            after = pl.ds(pl.multiple_of((base + ROWS) % SIDE, 8), 8)
            ahead = pl.ds(pl.multiple_of((base + SIDE - 8) % SIDE, 8), 8)
            for plane in range(4):
                edges[step, plane] = jnp.where(upper, slab[plane, :, after, :], slab[plane, :, ahead, :])

    def flag_copy(step):
        if step == 0:
            return pltpu.make_async_copy(flag, flags.at[q], f_rs)
        return remote(flag, flags.at[q], f_ss, f_rs, ring(step))

    took(fields, here.at[0])
    for step in range(8):
        first_copy(0, step).start()
    for copy in small:
        copy.wait()
    flag[...] = jnp.full(flag.shape, accept[0], jnp.int32)

    alive = [[(counts[4 * ((y + d) % 4) + i] > 0).astype(jnp.int32) for i in range(4)] for d in range(4)]
    before = [[sum(alive[d][:i], jnp.int32(0)) for i in range(4)] for d in range(4)]
    total = [sum(alive[d], jnp.int32(0)) for d in range(4)]
    mine = [jnp.int32(-1)] * 4
    for c in range(4):
        for i in range(4):
            mine[c] = jnp.where((alive[0][i] == 1) & (before[0][i] == c), i, mine[c])
    split_up = jnp.minimum(total[3], 4 - total[2])
    split = jnp.minimum(total[2], 4 - total[1])
    cum, parent = jnp.int32(0), [jnp.int32(0)] * SLOTS
    for r in range(16):
        cum = cum + counts[r]
        for s in range(SLOTS):
            parent[s] = parent[s] + (cum <= 4 * y + s).astype(jnp.int32)
    code = []
    for s in range(SLOTS):
        value = jnp.int32(0)
        for d in range(4):
            for i in range(4):
                k = before[d][i]
                if d == 0:
                    way = jnp.int32(i)
                elif d == 1:
                    way = 4 + k
                elif d == 3:
                    way = 8 + k
                else:
                    way = jnp.where(k < split, 12 + total[1] + k, 16 + total[3] + k - split)
                value = jnp.where(parent[s] == 4 * ((y + d) % 4) + i, way, value)
        code.append(value)

    def same(value, number):
        return jnp.full((2, 8, LANES), value, jnp.int32) == number

    def octet(t):
        turn, late = t % 4, t >= 8
        pair = jnp.where(late, 2 + t // 2 % 2, t // 4)
        outer = jnp.where(late, t < 12, turn < 2)
        piece = jnp.where(outer, t % 2 * 3, 1 + t % 2)
        return pair, pl.ds(pl.multiple_of(jnp.where(pair == 0, turn, piece) * 8, 8), 8)

    def assemble(t, forward):
        pair, rows = octet(jnp.minimum(t, CHUNKS - 1))
        for c in range(4):
            own_here = [same(mine[c], i) for i in range(4)]
            down_here = [same(total[0], c - f) for f in range(c + 1)]
            up_here = [same(split_up + c - total[0], f) for f in range(4)]
            for h in range(2):
                pieces = [own[pair, h, i, :, rows, :] for i in range(4)]
                if forward:
                    down, up = from_above[t - LAG, 0, h], from_below[t - LAG, 0, h]
                    for f in range(1, c + 1):
                        down = jnp.where(down_here[f], from_above[t - LAG, f, h], down)
                    for f in range(1, 4):
                        up = jnp.where(up_here[f], from_below[t - LAG, f, h], up)
                else:
                    down = up = pieces[0]
                for i in range(4):
                    down = jnp.where(own_here[i], pieces[i], down)
                    up = jnp.where(own_here[i], pieces[i], up)
                send_down[t, c, h] = down
                send_up[t, c, h] = up

    def up_copy(t):
        return remote(send_up.at[t], from_below.at[t], up_ss, m_rs.at[t], above)

    def down_copy(t):
        return remote(send_down.at[t], from_above.at[t], down_ss, m_rs.at[t], below)

    def pick(u):
        pair, rows = octet(u)
        for s in range(SLOTS):
            here_ = [same(code[s], k) for k in range(20)]
            for h in range(2):
                value = own[pair, h, 0, :, rows, :]
                for i in range(1, 4):
                    value = jnp.where(here_[i], own[pair, h, i, :, rows, :], value)
                for c in range(4):
                    value = jnp.where(here_[4 + c], from_above[u, c, h], value)
                    value = jnp.where(here_[8 + c], from_below[u, c, h], value)
                    value = jnp.where(here_[12 + c], from_above[u + LAG, c, h], value)
                    value = jnp.where(here_[16 + c], from_below[u + LAG, c, h], value)
                plane = 4 + pair if h == 0 else 11 - pair
                phi0[s, plane, :, rows, :] = value

    def z_copies(pair):
        return (
            remote(phi0.at[:, 4 + pair], phi0.at[:, 12 + pair], z_ss, z_rs.at[pair], z_last),
            remote(phi0.at[:, 11 - pair], phi0.at[:, 3 - pair], z_ss, z_rs.at[pair], z_next),
        )

    zm_copies = (
        remote(mom.at[:, 4], mom.at[:, 12], zm_ss, zm_rs, z_last),
        remote(mom.at[:, 11], mom.at[:, 3], zm_ss, zm_rs, z_next),
    )

    def row_copies(pair):
        copies = []
        for n, plane in enumerate((4 + pair, 11 - pair)):
            copies.append(remote(phi0.at[:, plane, :, first], phi0.at[:, plane, :, high], r_ss, r_rs.at[pair], ring(-1)))
            copies.append(remote(phi0.at[:, plane, :, last], phi0.at[:, plane, :, low], r_ss, r_rs.at[pair], ring(1)))
        return copies

    momenta_pair = mom.at[:, pl.ds(4, 2), :, inner]
    row_halo = phi0.at[:, pl.ds(4, 2), :, beside_inner]

    def tick(t, carry):
        @pl.when(t == 0)
        def _():
            for step in range(8):
                first_copy(1, step).start()

        @pl.when((t == 1) | (t == 2) | (t == 4))
        def _():
            for step in range(8):
                field_copy((t + 2) // 2, step).start()

        @pl.when((t == 0) | (t == 2))
        def _():
            took(own.at[0, :, :, :, pl.ds(0, 16)], a_rs.at[2 * t])

        @pl.when((t == 4) | (t == 8) | (t == 10))
        def _():
            pair = t // 4 + t // 10
            took(own.at[pair], a_rs.at[pair])

        @pl.when(t >= LAG)
        def _():
            took(own.at[0, 0], m_rs.at[t - LAG])

        @pl.when(t < LAG)
        def _():
            assemble(t, False)

        @pl.when((t >= LAG) & (t < MESSAGES))
        def _():
            assemble(t, True)

        @pl.when(t < MESSAGES)
        def _():
            up_copy(t).start()
            down_copy(t).start()

        @pl.when(t == 6)
        def _():
            took(slab, here.at[1])
            fill_edges()
            for step in range(8):
                edge_copy(step).start()
                flag_copy(step).start()

        @pl.when((t >= 8) & (t < 16) & (t % 2 == 0))
        def _():
            for step in range(8):
                momenta_copy((t - 8) // 2, step).start()

        @pl.when(t >= 2 * LAG)
        def _():
            pick(t - 2 * LAG)

        @pl.when((t == 2 * LAG + 3) | (t == 2 * LAG + 5) | (t == 2 * LAG + 9) | (t == 2 * LAG + 11))
        def _():
            for copy in row_copies((t - 2 * LAG - 1) // 3):
                copy.start()

        @pl.when((t == 2 * LAG + 5) | (t == 2 * LAG + 7))
        def _():
            pair = (t - 2 * LAG - 5) // 2
            took(row_halo, r_rs.at[pair])
            for copy in z_copies(pair):
                copy.start()

        @pl.when(t == 14)
        def _():
            took(mom.at[:, pl.ds(4, 8), :, beside_inner], ch_rs)
            took(momenta_pair, c_rs.at[0])
            for copy in zm_copies:
                copy.start()

        return carry

    lax.fori_loop(0, MESSAGES + LAG, tick, 0)

    for pair in range(1, PAIRS):
        took(momenta_pair, c_rs.at[pair])
    took(flags, f_rs)
    took(mom.at[:, pl.ds(0, 2)], zm_rs)
    took(mom.at[:, pl.ds(0, 2)], zm_ss)
    for pair in range(2):
        took(phi0.at[:, pl.ds(0, 2)], z_rs.at[pair])
    for pair in range(2, PAIRS):
        took(row_halo, r_rs.at[pair])

    def end_copies(k, s):
        src, n = (phi2, phi3)[k - 2].at[s], k - 2
        return (
            remote(src.at[0], sides.at[n, s, 1], d_ss, d_rs.at[n, s], z_last),
            remote(src.at[7], sides.at[n, s, 0], d_ss, d_rs.at[n, s], z_next),
        )

    PARTS = ((2, 2), (1, 1), (0, 1))

    def result_copy(s, h, part, away):
        first_plane, number = PARTS[part]
        src = done.at[s, pl.ds(8 - number - first_plane if h else first_plane, number)]
        dst = out.at[0, pl.ds(4 - number - first_plane if h else first_plane, number), rows_of(q)]
        if away:
            return remote(src, dst, e_ss, e_rs, place(4 * h + s, y, z))
        return pltpu.make_async_copy(src, dst, e_rs)

    def results(s, part):
        for h in range(2):
            @pl.when(q == 4 * h + s)
            def _():
                result_copy(s, h, part, False).start()

            @pl.when(q != 4 * h + s)
            def _():
                result_copy(s, h, part, True).start()

    tiles = range(ALL // 8)

    def spread(t):
        return pl.ds(t, 8, stride=ALL // 8)

    edge_lane = lax.broadcasted_iota(jnp.int32, (8, LANES), 1)
    first_lane, last_lane = edge_lane == 0, edge_lane == LANES - 1

    def natural(ref, plane):
        return [[ref[plane, n, spread(t), :] for t in tiles] for n in range(2)]

    def packed(ref, plane):
        return [[ref[plane, n, 8 * t:8 * t + 8, :] for t in tiles] for n in range(2)]

    def keep(ref, plane, values):
        for n in range(2):
            for t in tiles:
                ref[plane, n, 8 * t:8 * t + 8, :] = values[n][t]

    def each(act, *args):
        return [[act(*(arg[n][t] for arg in args)) for t in tiles] for n in range(2)]

    def kick(below_, centre, above_, scale):
        back = [[pltpu.roll(centre[n][t], 1, 1) for t in tiles] for n in range(2)]
        fore = [[pltpu.roll(centre[n][t], LANES - 1, 1) for t in tiles] for n in range(2)]
        result = [[], []]
        for n in range(2):
            for t in tiles:
                c = centre[n][t]
                ahead = centre[n][t - 1] if t > 0 else pltpu.roll(centre[n][-1], 1, 0)
                after = centre[n][t + 1] if t < len(tiles) - 1 else pltpu.roll(centre[n][0], 7, 0)
                left_ = jnp.where(first_lane, back[1 - n][t], back[n][t])
                right_ = jnp.where(last_lane, fore[1 - n][t], fore[n][t])
                beside = (below_[n][t] + above_[n][t]) + (ahead + after) + (left_ + right_)
                result[n].append((scale * 2.0 * KAPPA) * beside + c * (scale * (4.0 * LAMBDA - 2.0) - (scale * 4.0 * LAMBDA) * (c * c)))
        return result

    def finish(s, taken, plane, trio, move):
        push = kick(*trio, EPS * EPS)
        start = natural(phi0.at[s], 4 + plane)
        value = each(lambda c, m, f, b: jnp.where(taken, c + (m + f), b), trio[1], move, push, start)
        for n in range(2):
            for t in tiles:
                turned[plane, n, spread(t), :] = value[n][t]
            done[s, plane, :, n * LANES:(n + 1) * LANES] = turned[plane, n, :ROWS, :]

    def advance(trio, move, scale=EPS * EPS):
        push = kick(*trio, scale)
        move = each(lambda m, f: m + f, move, push)
        return move, each(lambda c, m: c + m, trio[1], move)

    def one_slot(n, carry):
        s = (n % 2) * 2 + n // 2
        taken = flags[s] == 1
        start, second, third, held = phi0.at[s], phi2.at[s], phi3.at[s], moves.at[s]
        trio = [None, natural(start, 2), natural(start, 3)]
        for plane in range(3, 13):
            trio = trio[1:] + [natural(start, plane + 1)]
            move = each(lambda m: EPS * m, natural(mom.at[s], plane))
            move, value = advance(trio, move, 0.5 * EPS * EPS)
            if 4 <= plane < 12:
                keep(held, plane - 4, move)
            keep(phi1, plane - 3, value)
        trio = [None, packed(phi1, 0), packed(phi1, 1)]
        for plane in range(8):
            trio = trio[1:] + [packed(phi1, plane + 2)]
            move, value = advance(trio, packed(held, plane))
            keep(held, plane, move)
            keep(second, plane, value)
        for copy in end_copies(2, s):
            copy.start()
        trio = [None, packed(second, 0), packed(second, 1)]
        for plane in range(1, 7):
            trio = trio[1:] + [packed(second, plane + 1)]
            move, value = advance(trio, packed(held, plane))
            keep(held, plane, move)
            keep(third, plane, value)
        trio = [None, packed(third, 1), packed(third, 2)]
        for plane in range(2, 6):
            trio = trio[1:] + [packed(third, plane + 1)]
            finish(s, taken, plane, trio, packed(held, plane))
        results(s, 0)
        return carry

    def next_planes(n, carry):
        s = (n % 2) * 2 + n // 2
        taken = flags[s] == 1
        second, third, held, beyond = phi2.at[s], phi3.at[s], moves.at[s], sides.at[0, s]
        took(sides.at[0, s], d_rs.at[0, s])
        for plane in (0, 7):
            inside = packed(second, 1 if plane == 0 else 6)
            move, value = advance([packed(beyond, plane // 7), packed(second, plane), inside], packed(held, plane))
            keep(held, plane, move)
            keep(third, plane, value)
        for copy in end_copies(3, s):
            copy.start()
        for plane in (1, 6):
            finish(s, taken, plane, [packed(third, plane + n_) for n_ in (-1, 0, 1)], packed(held, plane))
        results(s, 1)
        return carry

    def end_planes(n, carry):
        s = (n % 2) * 2 + n // 2
        taken = flags[s] == 1
        third, held, beyond = phi3.at[s], moves.at[s], sides.at[1, s]
        took(sides.at[1, s], d_rs.at[1, s])
        for plane in (0, 7):
            inside = packed(third, 1 if plane == 0 else 6)
            finish(s, taken, plane, [packed(beyond, plane // 7), packed(third, plane), inside], packed(held, plane))
        results(s, 2)
        return carry

    lax.fori_loop(0, SLOTS, one_slot, 0)
    lax.fori_loop(0, SLOTS, next_planes, 0)
    lax.fori_loop(0, SLOTS, end_planes, 0)

    seven = pl.ds(0, 7 * ROWS)
    took(fields.at[:, :, seven], a_ss)
    took(slab.at[:, :, seven], c_ss)
    took(edges.at[pl.ds(0, 7)], ch_ss)
    took(flags.at[pl.ds(0, 7)], f_ss)
    took(send_up, up_ss)
    took(send_down, down_ss)
    took(phi0.at[:, pl.ds(0, 4)], z_ss)
    took(phi0.at[:, pl.ds(4, 8), :, beside_inner], r_ss)
    took(sides, d_ss)
    took(out.at[0, :, seven], e_ss)
    took(out, e_rs)


def local(field, momenta, counts, accept):
    f32, dma = jnp.float32, pltpu.SemaphoreType.DMA
    message = (MESSAGES, 4, 2, 2, 8, LANES)
    plane = (2, ALL, LANES)
    return pl.pallas_call(
        kernel,
        out_shape=jax.ShapeDtypeStruct(field.shape, f32),
        in_specs=[
            pl.BlockSpec(memory_space=pltpu.HBM),
            pl.BlockSpec(memory_space=pltpu.HBM),
            pl.BlockSpec(memory_space=pl.ANY),
            pl.BlockSpec(memory_space=pl.ANY),
        ],
        out_specs=pl.BlockSpec(memory_space=pltpu.VMEM),
        scratch_shapes=[
            pltpu.VMEM((PAIRS, 2, SLOTS, 2, ROWS, LANES), f32),
            pltpu.VMEM(message, f32),
            pltpu.VMEM(message, f32),
            pltpu.VMEM(message, f32),
            pltpu.VMEM(message, f32),
            pltpu.VMEM((SLOTS, 16) + plane, f32),
            pltpu.VMEM((10,) + plane, f32),
            pltpu.VMEM((SLOTS, 8) + plane, f32),
            pltpu.VMEM((SLOTS, 8) + plane, f32),
            pltpu.VMEM((SLOTS, 16) + plane, f32),
            pltpu.VMEM((SLOTS, 8) + plane, f32),
            pltpu.VMEM((2, SLOTS, 2) + plane, f32),
            pltpu.VMEM((SLOTS, 8, ROWS, SIDE), f32),
            pltpu.VMEM((8,) + plane, f32),
            pltpu.VMEM((4, 2, SIDE, LANES), f32),
            pltpu.VMEM((4, 2, SIDE, LANES), f32),
            pltpu.VMEM((8, 4, 2, 8, LANES), f32),
            pltpu.VMEM((8, LANES), jnp.int32),
            pltpu.VMEM((8, 8, LANES), jnp.int32),
            dma, dma((PAIRS + 1,)), dma, dma((PAIRS,)), dma, dma, dma, dma,
            dma, dma, dma((MESSAGES,)),
            dma, dma((2,)), dma, dma,
            dma, dma((PAIRS,)), dma, dma((2, SLOTS)), dma, dma, dma((4,)),
            pltpu.SMEM((16,), jnp.int32),
            pltpu.SMEM((1,), jnp.int32),
        ],
        compiler_params=pltpu.CompilerParams(collective_id=0, has_side_effects=True, vmem_limit_bytes=52 * 1024 * 1024),
    )(field, momenta, counts, accept)


def solution(mesh):
    placed = (P("rep", "gz", None, None), P("rep", "gz", None, None), P(), P("rep"))
    return jax.shard_map(
        local, mesh=mesh, in_specs=placed, out_specs=P("rep", "gz", None, None), check_vma=False
    )
```
